32 devices in a mesh: groups: 2 (over y), seq: 8 (over z, x), section: 2 (over core).
Axes of the slice: x: 2, y: 2, z: 4, core: 2. Of those that a mesh axis runs over, the one named last changes fastest.
Arguments:
- skip_in: bfloat16 [2, 1024, 1536], P('groups', 'seq'), parts along dimension 0, may hold values from -6 to 6
- attn_gain: float32 [1536], replicated, may hold values from 0.25 to 1.75
- query_weight: bfloat16 [1536, 1024], P(None, 'section'), may hold values from -0.625 to 0.625
- kv_weight: bfloat16 [1536, 256], replicated, may hold values from -0.15625 to 0.15625
- pair_bias: float32 [2, 8, 32, 32], P('groups', 'section', 'seq'), parts along dimension 0, may hold values from -12 to 400
- out_weight: bfloat16 [1024, 1536], P('section'), may hold values from -0.1875 to 0.1875
- dec_gain: float32 [1536], replicated, may hold values from 0.25 to 1.75
- dec_weight: bfloat16 [5, 1536, 768], P(None, 'seq', 'section'), may hold values from -0.0625 to 0.0625
- dec_bias: float32 [768], P('section'), may hold values from -3 to 3
Outputs:
- decoded: bfloat16 [2, 1024, 768], P('groups', 'seq', 'section'), parts along dimension 0
The draws below stay inside these ranges and needn't reach their ends.
There are 2 independent parts, one for each index of `groups`. The reference program is written for one: setup_inputs(seed, part) draws one part's arguments, and reference() takes and returns one part's arrays. A program takes and returns all parts, laid end to end along the dimension named above; an argument that names none is the same for every part. Nothing has to cross between parts.
All inputs are finite; a program needn't handle non-finite values.
Results may differ from the reference program's by a relative error of at most 0.0095.
Values may be sent and summed in bfloat16 or wider, within the bound.
A program may use at most 64 MiB of HBM per device.

```python
import jax
import jax.numpy as jnp
from jax import lax

D = 1536
OUT = 768
HEADS = 8
HEAD = 128
KW = 5
PAIR = 16
SEQS = 1
SEQ_LEN = 1024
COARSE_LEN = 512


def draw_pair_bias(key, part):
    base_key = jax.random.fold_in(key, 11)
    sub_keys = jax.random.split(base_key, 1)
    cells = COARSE_LEN // PAIR
    shape = (SEQS, HEADS, cells, cells)
    return jnp.clip(2.0 * jax.random.normal(sub_keys[0], shape, jnp.float32), -12.0, 12.0)


def shard_levels(rng, shape, cuts, low, top_value):
    level, own = 1.0, jax.random.fold_in(rng, 6)
    for position, parts in cuts:
        heights = jnp.exp(jax.random.uniform(jax.random.fold_in(own, position), (parts,), jnp.float32, low / len(cuts), top_value / len(cuts)))
        level = level * jnp.repeat(heights, shape[position] // parts).reshape([-1 if axis == position else 1 for axis in range(len(shape))])
    return level


def noise(key, shape, deviation, limit, cuts=(), kind=jnp.bfloat16):
    array = jax.random.normal(key, shape, jnp.float32) * deviation
    if len(cuts) > 0:
        array = shard_levels(key, shape, cuts, -0.22, 0.18) * array
    return jnp.clip(array, min=-limit, max=limit).astype(kind)


def setup_inputs(seed: int = 0, part: int = 0) -> dict:
    key_of = jax.random.split(jax.random.key(seed), 10)
    part_keys = jax.random.split(jax.random.fold_in(key_of[9], part), 10)
    skip_in = noise(part_keys[0], (SEQS, SEQ_LEN, D), 1.0, 6.0, ((1, 8),))
    attn_gain = jnp.clip(1.0 + 0.15 * jax.random.normal(key_of[1], (D,), jnp.float32), 0.25, 1.75)
    query_weight = noise(key_of[2], (D, HEADS * HEAD), (D // 16) ** -0.5, 0.625, ((1, 2),))
    kv_weight = noise(key_of[3], (D, 2 * HEAD), D ** -0.5, 0.15625)
    pair_bias = draw_pair_bias(jax.random.fold_in(jax.random.fold_in(key_of[9], part), 71), part)
    out_weight = noise(key_of[5], (HEADS * HEAD, D), (HEADS * HEAD) ** -0.5, 0.1875, ((0, 2),))
    dec_gain = jnp.clip(1.0 + 0.15 * jax.random.normal(key_of[6], (D,), jnp.float32), 0.25, 1.75)
    dec_weight = noise(key_of[7], (KW, D, OUT), (KW * D) ** -0.5, 0.0625, ((1, 8), (2, 2)))
    dec_bias = noise(key_of[8], (OUT,), 0.5, 3.0, ((0, 2),), jnp.float32)
    return dict(skip_in=skip_in, attn_gain=attn_gain, query_weight=query_weight, kv_weight=kv_weight, pair_bias=pair_bias, out_weight=out_weight, dec_gain=dec_gain, dec_weight=dec_weight, dec_bias=dec_bias)


def norm_scale(values_in, gain):
    wide = values_in.astype(jnp.float32)
    return wide * lax.rsqrt(lax.optimization_barrier(jnp.mean(wide * wide, axis=-1, keepdims=True)) + 1e-06) * gain

def reference(skip_in, attn_gain, query_weight, kv_weight, pair_bias, out_weight, dec_gain, dec_weight, dec_bias):
    seq_count, seq_length, channels = skip_in.shape
    half_length = seq_length // 2
    pooled = lax.optimization_barrier(jnp.max(skip_in.reshape(seq_count, half_length, 2, channels), axis=2))
    normed = norm_scale(pooled, attn_gain).astype(jnp.bfloat16)
    flattened = normed.reshape(seq_count * half_length, channels)
    query_rows = jnp.dot(flattened, query_weight, preferred_element_type=jnp.float32).astype(jnp.bfloat16)
    query_rows = query_rows.reshape(seq_count, half_length, HEADS, HEAD)
    key_values = jnp.dot(flattened, kv_weight, preferred_element_type=jnp.float32).astype(jnp.bfloat16)
    key_values = key_values.reshape(seq_count, half_length, 2 * HEAD)
    query_block = min(512, half_length)
    block_count = half_length // query_block
    logit_scale = 1.0 / jnp.sqrt(jnp.float32(HEAD))

    def attend_block(flat_index):
        seq_index = flat_index // block_count
        block_index = flat_index % block_count
        seq_queries = lax.dynamic_index_in_dim(query_rows, seq_index, 0, keepdims=False)
        block_queries = lax.dynamic_slice_in_dim(seq_queries, (block_index * query_block).astype(jnp.int32), query_block, 0)
        seq_kv = lax.dynamic_index_in_dim(key_values, seq_index, 0, keepdims=False)
        key_rows = seq_kv[:, :HEAD].astype(jnp.float32)
        value_matrix = seq_kv[:, HEAD:].astype(jnp.float32)
        seq_bias = lax.dynamic_index_in_dim(pair_bias, seq_index, 0, keepdims=False)
        bias_rows = lax.dynamic_slice_in_dim(seq_bias, (block_index * (query_block // PAIR)).astype(jnp.int32), query_block // PAIR, 1)
        full_bias = jnp.repeat(jnp.repeat(bias_rows, PAIR, axis=1), PAIR, axis=2)
        scores = jnp.einsum('qhd,kd->hqk', block_queries.astype(jnp.float32), key_rows) * logit_scale + full_bias
        row_max = lax.optimization_barrier(jnp.max(scores, axis=-1, keepdims=True))
        exponent_scores = jnp.exp(scores - row_max)
        totals = lax.optimization_barrier(jnp.sum(exponent_scores, axis=-1))
        rounded = lax.optimization_barrier(exponent_scores.astype(jnp.bfloat16)).astype(jnp.float32)
        context = jnp.einsum('hqk,kd->qhd', rounded, value_matrix) / jnp.transpose(totals)[:, :, None]
        return context.astype(jnp.bfloat16).reshape(query_block, HEADS * HEAD)
    contexts = lax.map(attend_block, jnp.arange(seq_count * block_count, dtype=jnp.int32))
    contexts = contexts.reshape(seq_count * half_length, HEADS * HEAD)
    projected = jnp.dot(contexts, out_weight, preferred_element_type=jnp.float32).reshape(seq_count, half_length, channels)
    attended = (pooled.astype(jnp.float32) + projected).astype(jnp.bfloat16)
    joined = (jnp.repeat(attended, 2, axis=1).astype(jnp.float32) + skip_in.astype(jnp.float32)).astype(jnp.bfloat16)
    activated = jax.nn.gelu(norm_scale(joined, dec_gain)).astype(jnp.bfloat16)
    margin = KW // 2
    padded = jnp.pad(activated, ((0, 0), (margin, margin), (0, 0)))
    convolved = jnp.zeros((seq_count * seq_length, OUT), jnp.float32)
    for tap_index in range(KW):
        window = padded[:, tap_index:tap_index + seq_length].reshape(seq_count * seq_length, channels)
        convolved = convolved + jnp.dot(window, dec_weight[tap_index], preferred_element_type=jnp.float32)
    convolved = convolved.reshape(seq_count, seq_length, OUT)
    decoded = convolved + dec_bias + joined[:, :, :OUT].astype(jnp.float32)
    return decoded.astype(jnp.bfloat16)
```

```python
import functools
import math

import jax
import jax.numpy as jnp
from jax import lax
from jax.experimental import pallas as pl
from jax.experimental.pallas import tpu as pltpu
from jax.sharding import PartitionSpec as P

HEAD = 128
KW = 5
PAIR = 16


def extended(block, sides, width):
    for axis, dim in sides:
        count = lax.axis_size(axis)
        forward = [(i, i + 1) for i in range(count - 1)]
        backward = [(target, source) for source, target in forward]
        low = lax.ppermute(
            lax.slice_in_dim(block, block.shape[dim] - width, None, axis=dim), axis, forward
        )
        high = lax.ppermute(lax.slice_in_dim(block, 0, width, axis=dim), axis, backward)
        block = jnp.concatenate([low, block, high], axis=dim)
    return block


def norm_scale(values_in, gain):
    wide = values_in.astype(jnp.float32)
    return wide * lax.rsqrt(jnp.mean(wide * wide, axis=-1, keepdims=True) + 1e-06) * gain


def body(
    skip_in,
    attn_gain,
    query_weight,
    kv_weight,
    pair_bias,
    out_weight,
    dec_gain,
    dec_weight,
    dec_bias,
):
    seq_count, local_rows, channels = skip_in.shape
    half_rows = local_rows // 2
    local_heads = query_weight.shape[1] // HEAD
    logit_scale = 1.0 / math.sqrt(HEAD)
    pooled = jnp.max(skip_in.reshape(seq_count, half_rows, 2, channels), axis=2)
    normed = norm_scale(pooled, attn_gain).astype(jnp.bfloat16)
    flattened = normed.reshape(seq_count * half_rows, channels)
    query_rows = jnp.dot(flattened, query_weight, preferred_element_type=jnp.float32).astype(
        jnp.bfloat16
    )
    query_rows = query_rows.reshape(seq_count, half_rows, local_heads, HEAD)
    row_bias = jnp.repeat(pair_bias, PAIR, axis=2)
    row_bias = jnp.pad(row_bias, ((0, 0), (0, 0), (0, 0), (0, 2)))
    quarter = half_rows // 2
    own_rows = lax.dynamic_slice_in_dim(normed, lax.axis_index("section") * quarter, quarter, 1)
    key_values = jnp.dot(
        own_rows.reshape(seq_count * quarter, channels),
        kv_weight,
        preferred_element_type=jnp.float32,
    )
    key_values = key_values.astype(jnp.bfloat16).reshape(seq_count, quarter, 2 * HEAD)
    piece = lax.all_gather(key_values, ("seq", "section"), axis=1, tiled=True)
    start = jnp.int32(0)
    running_max = jnp.full((seq_count, local_heads, half_rows), -1e30, jnp.float32)
    running_sum = jnp.zeros((seq_count, local_heads, half_rows), jnp.float32)
    weighted = jnp.zeros((seq_count, local_heads, half_rows, HEAD), jnp.float32)
    piece_rows = piece.shape[1]
    block_size = min(piece_rows, 2048)
    for offset in range(0, piece_rows, block_size):
        piece_len = min(block_size, piece_rows - offset)
        sub_piece = piece[:, offset : offset + piece_len]
        key_portion = sub_piece[:, :, :HEAD]
        value_part = sub_piece[:, :, HEAD:]
        first_row = start + offset
        blocks = lax.dynamic_slice_in_dim(row_bias, first_row // PAIR, piece_len // PAIR + 2, 3)
        spread = jnp.repeat(blocks, PAIR, axis=3)
        key_bias = lax.dynamic_slice_in_dim(spread, first_row % PAIR, piece_len, 3)
        scores = (
            jnp.einsum(
                "wtzj,wgj->wztg", query_rows, key_portion, preferred_element_type=jnp.float32
            )
            * logit_scale
            + key_bias
        )
        new_max = jnp.maximum(running_max, jnp.max(scores, axis=-1))
        rescale = jnp.exp(running_max - new_max)
        exponent_scores = jnp.exp(scores - new_max[..., None])
        running_sum = running_sum * rescale + jnp.sum(exponent_scores, axis=-1)
        weighted = weighted * rescale[..., None] + jnp.einsum(
            "umrl,ult->umrt",
            exponent_scores.astype(jnp.bfloat16),
            value_part,
            preferred_element_type=jnp.float32,
        )
        running_max = new_max
    folded = (running_max, running_sum, weighted)
    running_max, running_sum, weighted = folded
    context = (weighted / running_sum[..., None]).astype(jnp.bfloat16)
    context = jnp.transpose(context, (0, 2, 1, 3)).reshape(
        seq_count * half_rows, local_heads * HEAD
    )
    partial_value = jnp.dot(context, out_weight, preferred_element_type=jnp.float32).reshape(
        seq_count, half_rows, channels
    )
    summed = lax.psum(partial_value.astype(jnp.bfloat16), "section").astype(jnp.float32)
    attended = (pooled.astype(jnp.float32) + summed).astype(jnp.bfloat16)
    joined = (
        jnp.repeat(attended, 2, axis=1).astype(jnp.float32) + skip_in.astype(jnp.float32)
    ).astype(jnp.bfloat16)
    activated = jax.nn.gelu(norm_scale(joined, dec_gain)).astype(jnp.bfloat16)
    padded = extended(activated, (("seq", 1),), KW // 2)
    out_half = dec_weight.shape[2]
    piece = lax.all_gather(dec_weight, "seq", axis=1, tiled=True)
    piece_rows = piece.shape[1]
    stacked = jnp.concatenate(
        [padded[:, tap_index : tap_index + local_rows] for tap_index in range(KW)], axis=2
    )
    stacked = stacked.reshape(seq_count * local_rows, KW * piece_rows)
    convolved = jnp.dot(
        stacked, piece.reshape(KW * piece_rows, out_half), preferred_element_type=jnp.float32
    )
    residual = lax.dynamic_slice_in_dim(joined, lax.axis_index("section") * out_half, out_half, 2)
    decoded = (
        convolved.reshape(seq_count, local_rows, out_half) + dec_bias + residual.astype(jnp.float32)
    )
    return decoded.astype(jnp.bfloat16)


def seq_pairs_fit(mesh, channels):
    pairs = mesh.shape["seq"] // 2
    return (
        mesh.shape["groups"] == 2
        and mesh.shape["section"] == 2
        and mesh.shape["seq"] % 2 == 0
        and pairs >= 2
        and channels % (pairs * 128) == 0
    )


def dot(a, b):
    return jnp.dot(a, b, preferred_element_type=jnp.float32)


def select_matrix(rows, cols, chosen):
    i = lax.broadcasted_iota(jnp.int32, (rows, cols), 0)
    j = lax.broadcasted_iota(jnp.int32, (rows, cols), 1)
    return jnp.where(chosen(i, j), 1.0, 0.0).astype(jnp.bfloat16)


def block_kernel(
    count,
    skip_ref,
    attn_gain_ref,
    wq_hbm,
    wkv_hbm,
    bias_ref,
    wout_hbm,
    dec_gain_ref,
    wdec_hbm,
    dec_bias_ref,
    out_ref,
    wq,
    wkv,
    wout,
    wdec,
    pooled_ref,
    kv,
    spread,
    partial,
    part_out,
    part_in,
    act,
    gathered,
    edges,
    padded,
    resid,
    resid_out,
    conv_out,
    conv_in,
    local_sem,
    kv_send,
    kv_recv,
    kvf_send,
    kvf_recv,
    w_send,
    w_recv,
    wf_send,
    wf_recv,
    sib_send,
    sib_recv,
    act_send,
    act_recv,
    actf_send,
    actf_recv,
    edge_send,
    edge_recv,
    conv_send,
    conv_recv,
):
    g, s, k = lax.axis_index("groups"), lax.axis_index("seq"), lax.axis_index("section")
    z, x = s // 2, s % 2
    pairs = count // 2
    local_rows, channels = skip_ref.shape
    half = local_rows // 2
    quarter = half // 2
    heads = wq.shape[1] // HEAD
    own_depth = wdec_hbm.shape[1]
    mid_depth = own_depth // 2
    out_half = wdec_hbm.shape[2]
    width = channels // pairs
    keys = kv.shape[0]
    sibling = (g, s, 1 - k)

    def remote(src, dst, send, recv, device):
        return pltpu.make_async_remote_copy(
            src_ref=src,
            dst_ref=dst,
            send_sem=send,
            recv_sem=recv,
            device_id=device,
            device_id_type=pl.DeviceIdType.MESH,
        )

    def at(start, size, step):
        return pl.ds(pl.multiple_of(start, step), size)

    loads = [
        pltpu.make_async_copy(wkv_hbm, wkv, local_sem.at[0]),
        pltpu.make_async_copy(wq_hbm, wq, local_sem.at[1]),
        pltpu.make_async_copy(wout_hbm, wout, local_sem.at[2]),
        pltpu.make_async_copy(
            wdec_hbm, wdec.at[:, at(x * own_depth, own_depth, 16)], local_sem.at[3]
        ),
    ]
    for load in loads:
        load.start()

    barrier = pltpu.get_barrier_semaphore()
    partners = [
        (g, lax.rem(s + step, count), lax.rem(k + core, 2))
        for step in range(count)
        for core in range(2)
        if step or core
    ] + [(1 - g, s, k)]
    for partner in partners:
        pl.semaphore_signal(
            barrier, inc=1, device_id=partner, device_id_type=pl.DeviceIdType.MESH
        )

    skip = skip_ref[...]
    pooled = jnp.maximum(
        dot(select_matrix(half, local_rows, lambda i, j: j == 2 * i), skip),
        dot(select_matrix(half, local_rows, lambda i, j: j == 2 * i + 1), skip),
    )
    pooled_ref[...] = pooled
    normed = norm_scale(pooled, attn_gain_ref[...]).astype(jnp.bfloat16)
    loads[0].wait()
    kv[at(s * half, half, 16), :] = dot(normed, wkv[...]).astype(jnp.bfloat16)

    pl.semaphore_wait(barrier, len(partners))

    def kv_rows(source, core):
        return kv.at[at(source * half + core * quarter, quarter, 16)]

    kv_copies = []
    for step in range(1, count):
        target = lax.rem(s + step, count)
        copy = remote(
            kv_rows(s, k), kv_rows(s, k), kv_send.at[step], kv_recv.at[step], (g, target, k)
        )
        copy.start()
        kv_copies.append(copy)

    pair = s + 1 - 2 * x
    other_base = (1 - x) * own_depth
    w_copies = []
    for tap in range(KW):
        copy = remote(
            wdec_hbm.at[tap, at(g * mid_depth, mid_depth, 16)],
            wdec.at[tap, at(x * own_depth + g * mid_depth, mid_depth, 16)],
            w_send.at[tap],
            w_recv.at[tap],
            (g, pair, k),
        )
        copy.start()
        w_copies.append(copy)
    wf_copies = []

    def pass_weight(tap):
        w_copies[tap].wait_recv()
        rows = wdec.at[tap, at(other_base + g * mid_depth, mid_depth, 16)]
        copy = remote(rows, rows, wf_send.at[tap], wf_recv.at[tap], (1 - g, s, k))
        copy.start()
        wf_copies.append(copy)

    loads[1].wait()
    queries = dot(normed, wq[...]).astype(jnp.bfloat16)
    queries = jnp.concatenate(
        [queries[:, h * HEAD : (h + 1) * HEAD] for h in range(heads)], axis=0
    )
    cells = bias_ref.shape[2]
    spreader = select_matrix(
        cells, keys, lambda i, j: jnp.logical_and(j >= PAIR * i, j < PAIR * i + PAIR)
    )
    for h in range(heads):
        rest = bias_ref[h]
        total = None
        for _ in range(3):
            term = rest.astype(jnp.bfloat16)
            rest = rest - term.astype(jnp.float32)
            wide = dot(term, spreader)
            total = wide if total is None else total + wide
        for cell in range(half // PAIR):
            spread[h * half + cell * PAIR : h * half + (cell + 1) * PAIR, :] = jnp.broadcast_to(
                total[cell : cell + 1, :], (PAIR, keys)
            )

    kvf_copies = []
    for step in range(1, count):
        kv_copies[step - 1].wait_recv()
        source = lax.rem(s - step + count, count)
        copy = remote(
            kv_rows(source, k),
            kv_rows(source, k),
            kvf_send.at[step],
            kvf_recv.at[step],
            sibling,
        )
        copy.start()
        kvf_copies.append(copy)
    for copy in kvf_copies:
        copy.wait_recv()
    for tap in range(3):
        pass_weight(tap)

    scores = lax.dot_general(
        queries,
        kv[:, :HEAD],
        (((1,), (1,)), ((), ())),
        preferred_element_type=jnp.float32,
    ) * (1.0 / math.sqrt(HEAD)) + spread[...]
    exponent = jnp.exp(scores - jnp.max(scores, axis=-1, keepdims=True))
    totals = jnp.sum(exponent, axis=-1, keepdims=True)
    context = (dot(exponent.astype(jnp.bfloat16), kv[:, HEAD:]) / totals).astype(jnp.bfloat16)
    context = jnp.concatenate([context[h * half : (h + 1) * half] for h in range(heads)], axis=1)
    loads[2].wait()
    partial[...] = dot(context, wout[...])

    part_out[...] = partial[at((1 - k) * quarter, quarter, 16), :].astype(jnp.bfloat16)
    part_copy = remote(part_out, part_in, sib_send.at[0], sib_recv.at[0], sibling)
    part_copy.start()
    for tap in range(3, KW):
        pass_weight(tap)
    part_copy.wait_recv()
    own = at(k * quarter, quarter, 16)
    attended = (
        pooled_ref[own, :] + (partial[own, :] + part_in[...].astype(jnp.float32))
    ).astype(jnp.bfloat16)
    repeater = select_matrix(
        half, quarter, lambda i, j: jnp.logical_or(i == 2 * j, i == 2 * j + 1)
    )
    own_rows = at(k * half, half, 16)
    joined = (dot(repeater, attended) + skip_ref[own_rows, :].astype(jnp.float32)).astype(
        jnp.bfloat16
    )
    activated = jax.nn.gelu(norm_scale(joined, dec_gain_ref[...])).astype(jnp.bfloat16)
    for chunk in range(pairs):
        act[chunk] = activated[:, chunk * width : (chunk + 1) * width]

    edge_copies = []
    for step in range(pairs):
        zz = lax.rem(z + step, pairs)
        for core in range(2):
            slot = step * 2 + core
            copy = remote(
                act.at[zz, at(k * (half - 16), 16, 16)],
                edges.at[k, z],
                edge_send.at[slot],
                edge_recv.at[k, z],
                (g, zz * 2 + 1 - x, core),
            )
            copy.start()
            edge_copies.append(copy)
    own_act = remote(
        act.at[z], gathered.at[z, own_rows], sib_send.at[1], sib_recv.at[1], sibling
    )
    own_act.start()
    act_copies = [None]
    for step in range(1, pairs):
        zz = lax.rem(z + step, pairs)
        copy = remote(
            act.at[zz],
            gathered.at[z, own_rows],
            act_send.at[step],
            act_recv.at[step],
            (g, zz * 2 + x, k),
        )
        copy.start()
        act_copies.append(copy)
    gathered[z, own_rows, :] = act[z]
    for section in range(2):
        resid_out[section] = joined[:, section * out_half : (section + 1) * out_half]
    resid_copy = remote(
        resid_out.at[1 - k], resid.at[own_rows], sib_send.at[2], sib_recv.at[2], sibling
    )
    resid_copy.start()
    resid[own_rows, :] = resid_out[k]

    actf_copies = [None]

    def pass_act(step):
        act_copies[step].wait_recv()
        zz = lax.rem(z - step + pairs, pairs)
        rows = gathered.at[zz, own_rows]
        copy = remote(rows, rows, actf_send.at[step], actf_recv.at[step], sibling)
        copy.start()
        actf_copies.append(copy)

    def convolve(zz):
        low = jnp.maximum(zz - 1 + x, 0)
        high = jnp.minimum(zz + x, pairs - 1)
        low_edge = edges[1, low].astype(jnp.float32)
        high_edge = edges[0, high].astype(jnp.float32)
        padded[0:16, :] = jnp.where(zz - 1 + x >= 0, low_edge, 0.0)
        padded[16 : 16 + local_rows, :] = gathered[zz].astype(jnp.float32)
        padded[16 + local_rows : 32 + local_rows, :] = jnp.where(
            zz + x < pairs, high_edge, 0.0
        )
        total = None
        for tap in range(KW):
            first = 16 + tap - KW // 2
            window = padded[first : first + local_rows, :].astype(jnp.bfloat16)
            term = dot(window, wdec[tap])
            total = term if total is None else total + term
        return total

    loads[3].wait()
    for copy in wf_copies:
        copy.wait_recv()
    own_act.wait_recv()
    for core in range(2):
        for zz in range(pairs):
            remote(
                act.at[0, pl.ds(0, 16)],
                edges.at[core, zz],
                edge_send.at[0],
                edge_recv.at[core, zz],
                sibling,
            ).wait_recv()
    pass_act(1)
    result = convolve(z)
    conv_copies = []
    for step in range(1, pairs):
        actf_copies[step].wait_recv()
        if step + 1 < pairs:
            pass_act(step + 1)
        zz = lax.rem(z - step + pairs, pairs)
        conv_out[step - 1] = convolve(zz).astype(jnp.bfloat16)
        copy = remote(
            conv_out.at[step - 1],
            conv_in.at[step - 1],
            conv_send.at[step],
            conv_recv.at[step],
            (g, zz * 2 + x, k),
        )
        copy.start()
        conv_copies.append(copy)
    resid_copy.wait_recv()
    result = result + dec_bias_ref[...] + resid[...].astype(jnp.float32)
    for step, copy in enumerate(conv_copies):
        copy.wait_recv()
        result = result + conv_in[step].astype(jnp.float32)
    out_ref[...] = result.astype(jnp.bfloat16)
    for copy in (
        kv_copies
        + kvf_copies
        + w_copies
        + wf_copies
        + [part_copy, own_act, resid_copy]
        + edge_copies
        + act_copies[1:]
        + actf_copies[1:]
        + conv_copies
    ):
        copy.wait_send()


def fused_body(
    count,
    skip_in,
    attn_gain,
    query_weight,
    kv_weight,
    pair_bias,
    out_weight,
    dec_gain,
    dec_weight,
    dec_bias,
):
    _, local_rows, channels = skip_in.shape
    half = local_rows // 2
    quarter = half // 2
    pairs = count // 2
    width = channels // pairs
    heads = query_weight.shape[1] // HEAD
    out_half = dec_weight.shape[2]
    keys = half * count
    bf16, f32 = jnp.bfloat16, jnp.float32
    vmem = pl.BlockSpec(memory_space=pltpu.VMEM)
    hbm = pl.BlockSpec(memory_space=pl.ANY)
    dma = pltpu.SemaphoreType.DMA
    scratch = [
        pltpu.VMEM(query_weight.shape, bf16),
        pltpu.VMEM(kv_weight.shape, bf16),
        pltpu.VMEM(out_weight.shape, bf16),
        pltpu.VMEM((KW, width, out_half), bf16),
        pltpu.VMEM((half, channels), f32),
        pltpu.VMEM((keys, 2 * HEAD), bf16),
        pltpu.VMEM((heads * half, keys), f32),
        pltpu.VMEM((half, channels), f32),
        pltpu.VMEM((quarter, channels), bf16),
        pltpu.VMEM((quarter, channels), bf16),
        pltpu.VMEM((pairs, half, width), bf16),
        pltpu.VMEM((pairs, local_rows, width), bf16),
        pltpu.VMEM((2, pairs, 16, width), bf16),
        pltpu.VMEM((local_rows + 32, width), f32),
        pltpu.VMEM((local_rows, out_half), bf16),
        pltpu.VMEM((2, half, out_half), bf16),
        pltpu.VMEM((pairs - 1, local_rows, out_half), bf16),
        pltpu.VMEM((pairs - 1, local_rows, out_half), bf16),
        dma((4,)),
        dma((count,)),
        dma((count,)),
        dma((count,)),
        dma((count,)),
        dma((KW,)),
        dma((KW,)),
        dma((KW,)),
        dma((KW,)),
        dma((3,)),
        dma((3,)),
        dma((pairs,)),
        dma((pairs,)),
        dma((pairs,)),
        dma((pairs,)),
        dma((2 * pairs,)),
        dma((2, pairs)),
        dma((pairs,)),
        dma((pairs,)),
    ]
    decoded = pl.pallas_call(
        functools.partial(block_kernel, count),
        out_shape=jax.ShapeDtypeStruct((local_rows, out_half), bf16),
        in_specs=[vmem, vmem, hbm, hbm, vmem, hbm, vmem, hbm, vmem],
        out_specs=vmem,
        scratch_shapes=scratch,
        compiler_params=pltpu.CompilerParams(
            collective_id=0, has_side_effects=True, vmem_limit_bytes=40 * 1024 * 1024
        ),
        cost_estimate=pl.CostEstimate(
            flops=2 * local_rows * KW * channels * out_half,
            bytes_accessed=6_000_000,
            transcendentals=heads * half * keys,
        ),
    )(
        skip_in[0],
        attn_gain.reshape(1, channels),
        query_weight,
        kv_weight,
        pair_bias[0],
        out_weight,
        dec_gain.reshape(1, channels),
        dec_weight,
        dec_bias.reshape(1, out_half),
    )
    return decoded[None]


def solution(mesh):
    def chosen(skip_in, *others):
        fits = skip_in.shape[0] == 1 and skip_in.shape[1] % 64 == 0
        if fits and seq_pairs_fit(mesh, skip_in.shape[2]):
            return fused_body(mesh.shape["seq"], skip_in, *others)
        return body(skip_in, *others)

    return jax.shard_map(
        chosen,
        mesh=mesh,
        in_specs=(
            P("groups", "seq", None),
            P(),
            P(None, "section"),
            P(),
            P("groups", "section", "seq", None),
            P("section", None),
            P(),
            P(None, "seq", "section"),
            P("section"),
        ),
        out_specs=P("groups", "seq", "section"),
        check_vma=False,
    )
```

```python
import functools
import math

import jax
import jax.numpy as jnp
from jax import lax
from jax.experimental import pallas as pl
from jax.experimental.pallas import tpu as pltpu
from jax.sharding import PartitionSpec as P

HEAD = 128
KW = 5
PAIR = 16


def extended(block, sides, width):
    for axis, dim in sides:
        count = lax.axis_size(axis)
        forward = [(i, i + 1) for i in range(count - 1)]
        backward = [(target, source) for source, target in forward]
        low = lax.ppermute(
            lax.slice_in_dim(block, block.shape[dim] - width, None, axis=dim), axis, forward
        )
        high = lax.ppermute(lax.slice_in_dim(block, 0, width, axis=dim), axis, backward)
        block = jnp.concatenate([low, block, high], axis=dim)
    return block


def norm_scale(values_in, gain):
    wide = values_in.astype(jnp.float32)
    return wide * lax.rsqrt(jnp.mean(wide * wide, axis=-1, keepdims=True) + 1e-06) * gain


def body(
    skip_in,
    attn_gain,
    query_weight,
    kv_weight,
    pair_bias,
    out_weight,
    dec_gain,
    dec_weight,
    dec_bias,
):
    seq_count, local_rows, channels = skip_in.shape
    half_rows = local_rows // 2
    local_heads = query_weight.shape[1] // HEAD
    logit_scale = 1.0 / math.sqrt(HEAD)
    pooled = jnp.max(skip_in.reshape(seq_count, half_rows, 2, channels), axis=2)
    normed = norm_scale(pooled, attn_gain).astype(jnp.bfloat16)
    flattened = normed.reshape(seq_count * half_rows, channels)
    query_rows = jnp.dot(flattened, query_weight, preferred_element_type=jnp.float32).astype(
        jnp.bfloat16
    )
    query_rows = query_rows.reshape(seq_count, half_rows, local_heads, HEAD)
    row_bias = jnp.repeat(pair_bias, PAIR, axis=2)
    row_bias = jnp.pad(row_bias, ((0, 0), (0, 0), (0, 0), (0, 2)))
    quarter = half_rows // 2
    own_rows = lax.dynamic_slice_in_dim(normed, lax.axis_index("section") * quarter, quarter, 1)
    key_values = jnp.dot(
        own_rows.reshape(seq_count * quarter, channels),
        kv_weight,
        preferred_element_type=jnp.float32,
    )
    key_values = key_values.astype(jnp.bfloat16).reshape(seq_count, quarter, 2 * HEAD)
    piece = lax.all_gather(key_values, ("seq", "section"), axis=1, tiled=True)
    start = jnp.int32(0)
    running_max = jnp.full((seq_count, local_heads, half_rows), -1e30, jnp.float32)
    running_sum = jnp.zeros((seq_count, local_heads, half_rows), jnp.float32)
    weighted = jnp.zeros((seq_count, local_heads, half_rows, HEAD), jnp.float32)
    piece_rows = piece.shape[1]
    block_size = min(piece_rows, 2048)
    for offset in range(0, piece_rows, block_size):
        piece_len = min(block_size, piece_rows - offset)
        sub_piece = piece[:, offset : offset + piece_len]
        key_portion = sub_piece[:, :, :HEAD]
        value_part = sub_piece[:, :, HEAD:]
        first_row = start + offset
        blocks = lax.dynamic_slice_in_dim(row_bias, first_row // PAIR, piece_len // PAIR + 2, 3)
        spread = jnp.repeat(blocks, PAIR, axis=3)
        key_bias = lax.dynamic_slice_in_dim(spread, first_row % PAIR, piece_len, 3)
        scores = (
            jnp.einsum(
                "wtzj,wgj->wztg", query_rows, key_portion, preferred_element_type=jnp.float32
            )
            * logit_scale
            + key_bias
        )
        new_max = jnp.maximum(running_max, jnp.max(scores, axis=-1))
        rescale = jnp.exp(running_max - new_max)
        exponent_scores = jnp.exp(scores - new_max[..., None])
        running_sum = running_sum * rescale + jnp.sum(exponent_scores, axis=-1)
        weighted = weighted * rescale[..., None] + jnp.einsum(
            "umrl,ult->umrt",
            exponent_scores.astype(jnp.bfloat16),
            value_part,
            preferred_element_type=jnp.float32,
        )
        running_max = new_max
    folded = (running_max, running_sum, weighted)
    running_max, running_sum, weighted = folded
    context = (weighted / running_sum[..., None]).astype(jnp.bfloat16)
    context = jnp.transpose(context, (0, 2, 1, 3)).reshape(
        seq_count * half_rows, local_heads * HEAD
    )
    partial_value = jnp.dot(context, out_weight, preferred_element_type=jnp.float32).reshape(
        seq_count, half_rows, channels
    )
    summed = lax.psum(partial_value.astype(jnp.bfloat16), "section").astype(jnp.float32)
    attended = (pooled.astype(jnp.float32) + summed).astype(jnp.bfloat16)
    joined = (
        jnp.repeat(attended, 2, axis=1).astype(jnp.float32) + skip_in.astype(jnp.float32)
    ).astype(jnp.bfloat16)
    activated = jax.nn.gelu(norm_scale(joined, dec_gain)).astype(jnp.bfloat16)
    padded = extended(activated, (("seq", 1),), KW // 2)
    out_half = dec_weight.shape[2]
    piece = lax.all_gather(dec_weight, "seq", axis=1, tiled=True)
    piece_rows = piece.shape[1]
    stacked = jnp.concatenate(
        [padded[:, tap_index : tap_index + local_rows] for tap_index in range(KW)], axis=2
    )
    stacked = stacked.reshape(seq_count * local_rows, KW * piece_rows)
    convolved = jnp.dot(
        stacked, piece.reshape(KW * piece_rows, out_half), preferred_element_type=jnp.float32
    )
    residual = lax.dynamic_slice_in_dim(joined, lax.axis_index("section") * out_half, out_half, 2)
    decoded = (
        convolved.reshape(seq_count, local_rows, out_half) + dec_bias + residual.astype(jnp.float32)
    )
    return decoded.astype(jnp.bfloat16)


def seq_pairs_fit(mesh, channels):
    pairs = mesh.shape["seq"] // 2
    return (
        mesh.shape["groups"] == 2
        and mesh.shape["section"] == 2
        and mesh.shape["seq"] % 2 == 0
        and pairs >= 2
        and channels % (pairs * 128) == 0
    )


def dot(a, b):
    return jnp.dot(a, b, preferred_element_type=jnp.float32)


def select_matrix(rows, cols, chosen):
    i = lax.broadcasted_iota(jnp.int32, (rows, cols), 0)
    j = lax.broadcasted_iota(jnp.int32, (rows, cols), 1)
    return jnp.where(chosen(i, j), 1.0, 0.0).astype(jnp.bfloat16)


def block_kernel(
    count,
    skip_hbm,
    attn_gain_hbm,
    wq_hbm,
    wkv_hbm,
    bias_hbm,
    wout_hbm,
    dec_gain_hbm,
    wdec_hbm,
    dec_bias_hbm,
    out_ref,
    skip_ref,
    attn_gain_ref,
    bias_ref,
    dec_gain_ref,
    dec_bias_ref,
    wq,
    wkv,
    wout,
    wdec,
    pooled_ref,
    kv,
    spread,
    partial,
    part_out,
    part_in,
    act,
    gathered,
    edges,
    outside,
    padded,
    resid,
    resid_out,
    conv_out,
    conv_in,
    local_sem,
    kv_send,
    kv_recv,
    kvf_send,
    kvf_recv,
    w_send,
    w_recv,
    wf_send,
    wf_recv,
    sib_send,
    sib_recv,
    act_send,
    act_recv,
    actf_send,
    actf_recv,
    edge_send,
    edge_recv,
    outside_send,
    outside_recv,
    conv_send,
    conv_recv,
):
    g, s, k = lax.axis_index("groups"), lax.axis_index("seq"), lax.axis_index("section")
    pairs = count // 2
    h, q = s // pairs, s % pairs
    _, local_rows, channels = skip_hbm.shape
    half = local_rows // 2
    quarter = half // 2
    heads = wq.shape[1] // HEAD
    own_depth = wdec_hbm.shape[1]
    mid_depth = own_depth // 2
    out_half = wdec_hbm.shape[2]
    width = channels // pairs
    keys = kv.shape[0]
    sibling = (g, s, 1 - k)

    def remote(src, dst, send, recv, device):
        return pltpu.make_async_remote_copy(
            src_ref=src,
            dst_ref=dst,
            send_sem=send,
            recv_sem=recv,
            device_id=device,
            device_id_type=pl.DeviceIdType.MESH,
        )

    def at(start, size, step):
        return pl.ds(pl.multiple_of(start, step), size)

    sources = [
        (skip_hbm, skip_ref),
        (attn_gain_hbm, attn_gain_ref),
        (wkv_hbm, wkv),
        (bias_hbm, bias_ref),
        (wq_hbm, wq),
        (wout_hbm, wout),
        (dec_gain_hbm, dec_gain_ref),
        (dec_bias_hbm, dec_bias_ref),
    ] + [
        (wdec_hbm.at[tap], wdec.at[at(tap * width + h * own_depth, own_depth, 16)])
        for tap in range(KW)
    ]
    loads = [
        pltpu.make_async_copy(src, dst, local_sem.at[slot])
        for slot, (src, dst) in enumerate(sources)
    ]
    for load in loads:
        load.start()

    barrier = pltpu.get_barrier_semaphore()
    partners = [
        (g, lax.rem(s + step, count), lax.rem(k + core, 2))
        for step in range(count)
        for core in range(2)
        if step or core
    ] + [(1 - g, s, k)]
    for partner in partners:
        pl.semaphore_signal(
            barrier, inc=1, device_id=partner, device_id_type=pl.DeviceIdType.MESH
        )

    loads[0].wait()
    skip = skip_ref[0]
    pooled = jnp.maximum(
        dot(select_matrix(half, local_rows, lambda i, j: j == 2 * i), skip),
        dot(select_matrix(half, local_rows, lambda i, j: j == 2 * i + 1), skip),
    )
    pooled_ref[...] = pooled
    loads[1].wait()
    normed = norm_scale(pooled, attn_gain_ref[...][None, :]).astype(jnp.bfloat16)
    loads[2].wait()
    kv[at(s * half, half, 16), :] = dot(normed, wkv[...]).astype(jnp.bfloat16)

    pl.semaphore_wait(barrier, len(partners))

    def kv_rows(source, core):
        return kv.at[at(source * half + core * quarter, quarter, 16)]

    kv_copies = []
    for step in range(1, count):
        target = lax.rem(s + step, count)
        copy = remote(
            kv_rows(s, k), kv_rows(s, k), kv_send.at[step], kv_recv.at[step], (g, target, k)
        )
        copy.start()
        kv_copies.append(copy)

    pair = lax.rem(s + pairs, count)
    other_base = (1 - h) * own_depth
    w_copies = []
    for tap in range(KW):
        copy = remote(
            wdec_hbm.at[tap, at(g * mid_depth, mid_depth, 16)],
            wdec.at[at(tap * width + h * own_depth + g * mid_depth, mid_depth, 16)],
            w_send.at[tap],
            w_recv.at[tap],
            (g, pair, k),
        )
        copy.start()
        w_copies.append(copy)
    wf_copies = []

    def pass_weight(tap):
        w_copies[tap].wait_recv()
        rows = wdec.at[at(tap * width + other_base + g * mid_depth, mid_depth, 16)]
        copy = remote(rows, rows, wf_send.at[tap], wf_recv.at[tap], (1 - g, s, k))
        copy.start()
        wf_copies.append(copy)

    loads[4].wait()
    queries = dot(normed, wq[...]).astype(jnp.bfloat16)
    queries = jnp.concatenate(
        [queries[:, i * HEAD : (i + 1) * HEAD] for i in range(heads)], axis=0
    )
    loads[3].wait()
    cells = bias_ref.shape[3]
    spreader = select_matrix(
        cells, keys, lambda i, j: jnp.logical_and(j >= PAIR * i, j < PAIR * i + PAIR)
    )
    for head in range(heads):
        rest = bias_ref[0, head]
        total = None
        for _ in range(3):
            term = rest.astype(jnp.bfloat16)
            rest = rest - term.astype(jnp.float32)
            wide = dot(term, spreader)
            total = wide if total is None else total + wide
        for cell in range(half // PAIR):
            first = head * half + cell * PAIR
            spread[first : first + PAIR, :] = jnp.broadcast_to(
                total[cell : cell + 1, :], (PAIR, keys)
            )

    kvf_copies = []
    for step in range(1, count):
        kv_copies[step - 1].wait_recv()
        source = lax.rem(s - step + count, count)
        copy = remote(
            kv_rows(source, k),
            kv_rows(source, k),
            kvf_send.at[step],
            kvf_recv.at[step],
            sibling,
        )
        copy.start()
        kvf_copies.append(copy)
    for copy in kvf_copies:
        copy.wait_recv()
    pass_weight(0)

    scores = lax.dot_general(
        queries,
        kv[:, :HEAD],
        (((1,), (1,)), ((), ())),
        preferred_element_type=jnp.float32,
    ) * (1.0 / math.sqrt(HEAD)) + spread[...]
    exponent = jnp.exp(scores - jnp.max(scores, axis=-1, keepdims=True))
    totals = jnp.sum(exponent, axis=-1, keepdims=True)
    context = (dot(exponent.astype(jnp.bfloat16), kv[:, HEAD:]) / totals).astype(jnp.bfloat16)
    context = jnp.concatenate([context[i * half : (i + 1) * half] for i in range(heads)], axis=1)
    loads[5].wait()
    partial[...] = dot(context, wout[...])

    part_out[...] = partial[at((1 - k) * quarter, quarter, 16), :].astype(jnp.bfloat16)
    part_copy = remote(part_out, part_in, sib_send.at[0], sib_recv.at[0], sibling)
    part_copy.start()
    pass_weight(1)
    part_copy.wait_recv()
    own = at(k * quarter, quarter, 16)
    attended = (
        pooled_ref[own, :] + (partial[own, :] + part_in[...].astype(jnp.float32))
    ).astype(jnp.bfloat16)
    repeater = select_matrix(
        half, quarter, lambda i, j: jnp.logical_or(i == 2 * j, i == 2 * j + 1)
    )
    own_rows = at(k * half, half, 16)
    joined = (dot(repeater, attended) + skip_ref[0, own_rows, :].astype(jnp.float32)).astype(
        jnp.bfloat16
    )
    loads[6].wait()
    activated = jax.nn.gelu(norm_scale(joined, dec_gain_ref[...][None, :])).astype(jnp.bfloat16)
    for chunk in range(pairs):
        act[chunk] = jnp.concatenate(
            [
                activated[:, (chunk + i * pairs) * own_depth : (chunk + i * pairs + 1) * own_depth]
                for i in range(2)
            ],
            axis=1,
        )

    edge_rows = at(k * (half - 16), 16, 16)
    edge_copies = []
    for step in range(pairs):
        target = lax.rem(q + step, pairs)
        for core in range(2):
            if step == 0 and core == 0:
                continue
            slot = step * 2 + core
            copy = remote(
                act.at[target, edge_rows],
                edges.at[k, q],
                edge_send.at[slot],
                edge_recv.at[k, q],
                (g, h * pairs + target, lax.rem(k + core, 2)),
            )
            copy.start()
            edge_copies.append(copy)
    edges[k, q] = act[q, edge_rows, :]
    meets = jnp.logical_or(
        jnp.logical_and(s == pairs - 1, k == 1), jnp.logical_and(s == pairs, k == 0)
    )
    outside_copies = [
        remote(
            act.at[target, edge_rows],
            outside,
            outside_send.at[target * 2 + core],
            outside_recv.at[0],
            (g, (1 - h) * pairs + target, core),
        )
        for target in range(pairs)
        for core in range(2)
    ]

    @pl.when(meets)
    def _():
        for copy in outside_copies:
            copy.start()

    own_act = remote(
        act.at[q], gathered.at[q, own_rows], sib_send.at[1], sib_recv.at[1], sibling
    )
    own_act.start()
    act_copies = [None]
    for step in range(1, pairs):
        target = lax.rem(q + step, pairs)
        copy = remote(
            act.at[target],
            gathered.at[q, own_rows],
            act_send.at[step],
            act_recv.at[step],
            (g, h * pairs + target, k),
        )
        copy.start()
        act_copies.append(copy)
    gathered[q, own_rows, :] = act[q]
    for section in range(2):
        resid_out[section] = joined[:, section * out_half : (section + 1) * out_half]
    resid_copy = remote(
        resid_out.at[1 - k], resid.at[own_rows], sib_send.at[2], sib_recv.at[2], sibling
    )
    resid_copy.start()
    resid[own_rows, :] = resid_out[k]

    actf_copies = [None]

    def pass_act(step):
        act_copies[step].wait_recv()
        rows = gathered.at[lax.rem(q - step + pairs, pairs), own_rows]
        copy = remote(rows, rows, actf_send.at[step], actf_recv.at[step], sibling)
        copy.start()
        actf_copies.append(copy)

    def convolve(block):
        outer = outside[...].astype(jnp.float32)
        low = edges[1, jnp.maximum(block - 1, 0)].astype(jnp.float32)
        low_outer = jnp.where(h == 1, outer, 0.0)
        high = edges[0, jnp.minimum(block + 1, pairs - 1)].astype(jnp.float32)
        high_outer = jnp.where(h == 0, outer, 0.0)
        padded[0:16, :] = jnp.where(block == 0, low_outer, low)
        padded[16 : 16 + local_rows, :] = gathered[block].astype(jnp.float32)
        padded[16 + local_rows : 32 + local_rows, :] = jnp.where(
            block == pairs - 1, high_outer, high
        )
        windows = []
        for tap in range(KW):
            first = 16 + tap - KW // 2
            windows.append(padded[first : first + local_rows, :].astype(jnp.bfloat16))
        return dot(jnp.concatenate(windows, axis=1), wdec[...])

    pass_weight(2)
    pass_weight(3)
    own_act.wait_recv()
    for core in range(2):
        for block in range(pairs):

            @pl.when(jnp.logical_or(block != q, core != k))
            def _():
                remote(
                    act.at[0, pl.ds(0, 16)],
                    edges.at[core, block],
                    edge_send.at[0],
                    edge_recv.at[core, block],
                    sibling,
                ).wait_recv()

    outside_copies[0].wait_recv()
    pass_weight(4)
    for load in loads[7:]:
        load.wait()
    for copy in wf_copies:
        copy.wait_recv()
    pass_act(1)
    result = convolve(q)
    conv_copies = []
    for step in range(1, pairs):
        actf_copies[step].wait_recv()
        if step + 1 < pairs:
            pass_act(step + 1)
        block = lax.rem(q - step + pairs, pairs)
        conv_out[step - 1] = convolve(block).astype(jnp.bfloat16)
        copy = remote(
            conv_out.at[step - 1],
            conv_in.at[step - 1],
            conv_send.at[step],
            conv_recv.at[step],
            (g, h * pairs + block, k),
        )
        copy.start()
        conv_copies.append(copy)
    resid_copy.wait_recv()
    result = result + dec_bias_ref[...][None, :] + resid[...].astype(jnp.float32)
    for step, copy in enumerate(conv_copies):
        copy.wait_recv()
        result = result + conv_in[step].astype(jnp.float32)
    out_ref[...] = result.astype(jnp.bfloat16)
    for copy in (
        kv_copies
        + kvf_copies
        + w_copies
        + wf_copies
        + [part_copy, own_act, resid_copy]
        + edge_copies
        + act_copies[1:]
        + actf_copies[1:]
        + conv_copies
    ):
        copy.wait_send()

    @pl.when(meets)
    def _():
        for copy in outside_copies:
            copy.wait_send()


def fused_body(
    count,
    skip_in,
    attn_gain,
    query_weight,
    kv_weight,
    pair_bias,
    out_weight,
    dec_gain,
    dec_weight,
    dec_bias,
):
    _, local_rows, channels = skip_in.shape
    half = local_rows // 2
    quarter = half // 2
    pairs = count // 2
    width = channels // pairs
    heads = query_weight.shape[1] // HEAD
    out_half = dec_weight.shape[2]
    keys = half * count
    bf16, f32 = jnp.bfloat16, jnp.float32
    hbm = pl.BlockSpec(memory_space=pltpu.HBM)
    dma = pltpu.SemaphoreType.DMA
    scratch = [
        pltpu.VMEM(skip_in.shape, bf16),
        pltpu.VMEM(attn_gain.shape, f32),
        pltpu.VMEM(pair_bias.shape, f32),
        pltpu.VMEM(dec_gain.shape, f32),
        pltpu.VMEM(dec_bias.shape, f32),
        pltpu.VMEM(query_weight.shape, bf16),
        pltpu.VMEM(kv_weight.shape, bf16),
        pltpu.VMEM(out_weight.shape, bf16),
        pltpu.VMEM((KW * width, out_half), bf16),
        pltpu.VMEM((half, channels), f32),
        pltpu.VMEM((keys, 2 * HEAD), bf16),
        pltpu.VMEM((heads * half, keys), f32),
        pltpu.VMEM((half, channels), f32),
        pltpu.VMEM((quarter, channels), bf16),
        pltpu.VMEM((quarter, channels), bf16),
        pltpu.VMEM((pairs, half, width), bf16),
        pltpu.VMEM((pairs, local_rows, width), bf16),
        pltpu.VMEM((2, pairs, 16, width), bf16),
        pltpu.VMEM((16, width), bf16),
        pltpu.VMEM((local_rows + 32, width), f32),
        pltpu.VMEM((local_rows, out_half), bf16),
        pltpu.VMEM((2, half, out_half), bf16),
        pltpu.VMEM((pairs - 1, local_rows, out_half), bf16),
        pltpu.VMEM((pairs - 1, local_rows, out_half), bf16),
        dma((8 + KW,)),
        dma((count,)),
        dma((count,)),
        dma((count,)),
        dma((count,)),
        dma((KW,)),
        dma((KW,)),
        dma((KW,)),
        dma((KW,)),
        dma((3,)),
        dma((3,)),
        dma((pairs,)),
        dma((pairs,)),
        dma((pairs,)),
        dma((pairs,)),
        dma((2 * pairs,)),
        dma((2, pairs)),
        dma((2 * pairs,)),
        dma((1,)),
        dma((pairs,)),
        dma((pairs,)),
    ]
    decoded = pl.pallas_call(
        functools.partial(block_kernel, count),
        out_shape=jax.ShapeDtypeStruct((local_rows, out_half), bf16),
        in_specs=[hbm] * 9,
        out_specs=pl.BlockSpec(memory_space=pltpu.VMEM),
        scratch_shapes=scratch,
        compiler_params=pltpu.CompilerParams(
            collective_id=0, has_side_effects=True, vmem_limit_bytes=63 * 1024 * 1024
        ),
        cost_estimate=pl.CostEstimate(
            flops=2 * local_rows * KW * channels * out_half,
            bytes_accessed=6_000_000,
            transcendentals=heads * half * keys,
        ),
    )(
        skip_in,
        attn_gain,
        query_weight,
        kv_weight,
        pair_bias,
        out_weight,
        dec_gain,
        dec_weight,
        dec_bias,
    )
    return decoded[None]


def solution(mesh):
    def chosen(skip_in, *others):
        fits = skip_in.shape[0] == 1 and skip_in.shape[1] % 64 == 0
        if fits and seq_pairs_fit(mesh, skip_in.shape[2]):
            return fused_body(mesh.shape["seq"], skip_in, *others)
        return body(skip_in, *others)

    return jax.shard_map(
        chosen,
        mesh=mesh,
        in_specs=(
            P("groups", "seq", None),
            P(),
            P(None, "section"),
            P(),
            P("groups", "section", "seq", None),
            P("section", None),
            P(),
            P(None, "seq", "section"),
            P("section"),
        ),
        out_specs=P("groups", "seq", "section"),
        check_vma=False,
    )
```

```python
import functools
import math

import jax
import jax.numpy as jnp
from jax import lax
from jax.experimental import pallas as pl
from jax.experimental.pallas import tpu as pltpu
from jax.sharding import PartitionSpec as P

HEAD = 128
KW = 5
PAIR = 16


def extended(block, sides, width):
    for axis, dim in sides:
        count = lax.axis_size(axis)
        forward = [(i, i + 1) for i in range(count - 1)]
        backward = [(target, source) for source, target in forward]
        low = lax.ppermute(
            lax.slice_in_dim(block, block.shape[dim] - width, None, axis=dim), axis, forward
        )
        high = lax.ppermute(lax.slice_in_dim(block, 0, width, axis=dim), axis, backward)
        block = jnp.concatenate([low, block, high], axis=dim)
    return block


def norm_scale(values_in, gain):
    wide = values_in.astype(jnp.float32)
    return wide * lax.rsqrt(jnp.mean(wide * wide, axis=-1, keepdims=True) + 1e-06) * gain


def body(
    skip_in,
    attn_gain,
    query_weight,
    kv_weight,
    pair_bias,
    out_weight,
    dec_gain,
    dec_weight,
    dec_bias,
):
    seq_count, local_rows, channels = skip_in.shape
    half_rows = local_rows // 2
    local_heads = query_weight.shape[1] // HEAD
    logit_scale = 1.0 / math.sqrt(HEAD)
    pooled = jnp.max(skip_in.reshape(seq_count, half_rows, 2, channels), axis=2)
    normed = norm_scale(pooled, attn_gain).astype(jnp.bfloat16)
    flattened = normed.reshape(seq_count * half_rows, channels)
    query_rows = jnp.dot(flattened, query_weight, preferred_element_type=jnp.float32).astype(
        jnp.bfloat16
    )
    query_rows = query_rows.reshape(seq_count, half_rows, local_heads, HEAD)
    row_bias = jnp.repeat(pair_bias, PAIR, axis=2)
    row_bias = jnp.pad(row_bias, ((0, 0), (0, 0), (0, 0), (0, 2)))
    quarter = half_rows // 2
    own_rows = lax.dynamic_slice_in_dim(normed, lax.axis_index("section") * quarter, quarter, 1)
    key_values = jnp.dot(
        own_rows.reshape(seq_count * quarter, channels),
        kv_weight,
        preferred_element_type=jnp.float32,
    )
    key_values = key_values.astype(jnp.bfloat16).reshape(seq_count, quarter, 2 * HEAD)
    piece = lax.all_gather(key_values, ("seq", "section"), axis=1, tiled=True)
    start = jnp.int32(0)
    running_max = jnp.full((seq_count, local_heads, half_rows), -1e30, jnp.float32)
    running_sum = jnp.zeros((seq_count, local_heads, half_rows), jnp.float32)
    weighted = jnp.zeros((seq_count, local_heads, half_rows, HEAD), jnp.float32)
    piece_rows = piece.shape[1]
    block_size = min(piece_rows, 2048)
    for offset in range(0, piece_rows, block_size):
        piece_len = min(block_size, piece_rows - offset)
        sub_piece = piece[:, offset : offset + piece_len]
        key_portion = sub_piece[:, :, :HEAD]
        value_part = sub_piece[:, :, HEAD:]
        first_row = start + offset
        blocks = lax.dynamic_slice_in_dim(row_bias, first_row // PAIR, piece_len // PAIR + 2, 3)
        spread = jnp.repeat(blocks, PAIR, axis=3)
        key_bias = lax.dynamic_slice_in_dim(spread, first_row % PAIR, piece_len, 3)
        scores = (
            jnp.einsum(
                "wtzj,wgj->wztg", query_rows, key_portion, preferred_element_type=jnp.float32
            )
            * logit_scale
            + key_bias
        )
        new_max = jnp.maximum(running_max, jnp.max(scores, axis=-1))
        rescale = jnp.exp(running_max - new_max)
        exponent_scores = jnp.exp(scores - new_max[..., None])
        running_sum = running_sum * rescale + jnp.sum(exponent_scores, axis=-1)
        weighted = weighted * rescale[..., None] + jnp.einsum(
            "umrl,ult->umrt",
            exponent_scores.astype(jnp.bfloat16),
            value_part,
            preferred_element_type=jnp.float32,
        )
        running_max = new_max
    folded = (running_max, running_sum, weighted)
    running_max, running_sum, weighted = folded
    context = (weighted / running_sum[..., None]).astype(jnp.bfloat16)
    context = jnp.transpose(context, (0, 2, 1, 3)).reshape(
        seq_count * half_rows, local_heads * HEAD
    )
    partial_value = jnp.dot(context, out_weight, preferred_element_type=jnp.float32).reshape(
        seq_count, half_rows, channels
    )
    summed = lax.psum(partial_value.astype(jnp.bfloat16), "section").astype(jnp.float32)
    attended = (pooled.astype(jnp.float32) + summed).astype(jnp.bfloat16)
    joined = (
        jnp.repeat(attended, 2, axis=1).astype(jnp.float32) + skip_in.astype(jnp.float32)
    ).astype(jnp.bfloat16)
    activated = jax.nn.gelu(norm_scale(joined, dec_gain)).astype(jnp.bfloat16)
    padded = extended(activated, (("seq", 1),), KW // 2)
    out_half = dec_weight.shape[2]
    piece = lax.all_gather(dec_weight, "seq", axis=1, tiled=True)
    piece_rows = piece.shape[1]
    stacked = jnp.concatenate(
        [padded[:, tap_index : tap_index + local_rows] for tap_index in range(KW)], axis=2
    )
    stacked = stacked.reshape(seq_count * local_rows, KW * piece_rows)
    convolved = jnp.dot(
        stacked, piece.reshape(KW * piece_rows, out_half), preferred_element_type=jnp.float32
    )
    residual = lax.dynamic_slice_in_dim(joined, lax.axis_index("section") * out_half, out_half, 2)
    decoded = (
        convolved.reshape(seq_count, local_rows, out_half) + dec_bias + residual.astype(jnp.float32)
    )
    return decoded.astype(jnp.bfloat16)


def seq_pairs_fit(mesh, channels):
    pairs = mesh.shape["seq"] // 2
    return (
        mesh.shape["groups"] == 2
        and mesh.shape["section"] == 2
        and mesh.shape["seq"] % 2 == 0
        and pairs >= 2
        and pairs & (pairs - 1) == 0
        and channels % (pairs * 128) == 0
    )


def dot(a, b):
    return jnp.dot(a, b, preferred_element_type=jnp.float32)


def select_matrix(rows, cols, chosen):
    i = lax.broadcasted_iota(jnp.int32, (rows, cols), 0)
    j = lax.broadcasted_iota(jnp.int32, (rows, cols), 1)
    return jnp.where(chosen(i, j), 1.0, 0.0).astype(jnp.bfloat16)


def block_kernel(
    count,
    skip_hbm,
    attn_gain_hbm,
    wq_hbm,
    wkv_hbm,
    bias_hbm,
    wout_hbm,
    dec_gain_hbm,
    wdec_hbm,
    dec_bias_hbm,
    out_ref,
    skip_ref,
    attn_gain_ref,
    bias_ref,
    dec_gain_ref,
    dec_bias_ref,
    wq,
    wkv,
    wout,
    wdec,
    pooled_ref,
    kv,
    spread,
    partial,
    part_out,
    part_in,
    act,
    gathered,
    edges,
    padded,
    resid,
    resid_out,
    conv_out,
    conv_in,
    local_sem,
    kv_send,
    kv_recv,
    kvf_send,
    kvf_recv,
    w_send,
    w_recv,
    wf_send,
    wf_recv,
    sib_send,
    sib_recv,
    act_send,
    act_recv,
    actf_send,
    actf_recv,
    edge_send,
    edge_recv,
    conv_send,
    conv_recv,
):
    g, s, k = lax.axis_index("groups"), lax.axis_index("seq"), lax.axis_index("section")
    pairs = count // 2
    z, x = s // 2, s % 2
    _, local_rows, channels = skip_hbm.shape
    half = local_rows // 2
    quarter = half // 2
    heads = wq.shape[1] // HEAD
    own_depth = wdec_hbm.shape[1]
    mid_depth = own_depth // 2
    out_half = wdec_hbm.shape[2]
    width = channels // pairs
    keys = kv.shape[0]
    sibling = (g, s, 1 - k)

    def remote(src, dst, send, recv, device):
        return pltpu.make_async_remote_copy(
            src_ref=src,
            dst_ref=dst,
            send_sem=send,
            recv_sem=recv,
            device_id=device,
            device_id_type=pl.DeviceIdType.MESH,
        )

    def at(start, size, step):
        return pl.ds(pl.multiple_of(start, step), size)

    sources = [
        (skip_hbm, skip_ref),
        (attn_gain_hbm, attn_gain_ref),
        (wkv_hbm, wkv),
        (bias_hbm, bias_ref),
        (wq_hbm, wq),
        (wout_hbm, wout),
        (dec_gain_hbm, dec_gain_ref),
        (dec_bias_hbm, dec_bias_ref),
    ] + [
        (wdec_hbm.at[tap], wdec.at[at(tap * width + x * own_depth, own_depth, 16)])
        for tap in range(KW)
    ]
    loads = [
        pltpu.make_async_copy(src, dst, local_sem.at[slot])
        for slot, (src, dst) in enumerate(sources)
    ]
    for load in loads[:3]:
        load.start()

    barrier = pltpu.get_barrier_semaphore()
    partners = [
        (g, lax.rem(s + step, count), lax.rem(k + core, 2))
        for step in range(count)
        for core in range(2)
        if step or core
    ] + [(1 - g, s, k)]
    for partner in partners:
        pl.semaphore_signal(
            barrier, inc=1, device_id=partner, device_id_type=pl.DeviceIdType.MESH
        )

    loads[0].wait()
    for load in loads[3:]:
        load.start()
    skip = skip_ref[0]
    pooled = jnp.maximum(
        dot(select_matrix(half, local_rows, lambda i, j: j == 2 * i), skip),
        dot(select_matrix(half, local_rows, lambda i, j: j == 2 * i + 1), skip),
    )
    pooled_ref[...] = pooled
    loads[1].wait()
    normed = norm_scale(pooled, attn_gain_ref[...][None, :]).astype(jnp.bfloat16)
    loads[2].wait()
    kv[at(s * half, half, 16), :] = dot(normed, wkv[...]).astype(jnp.bfloat16)

    pl.semaphore_wait(barrier, len(partners))

    def kv_rows(source, core):
        return kv.at[at(source * half + core * quarter, quarter, 16)]

    kv_copies = []
    for step in range(1, count):
        target = lax.rem(s + step, count)
        copy = remote(
            kv_rows(s, k), kv_rows(s, k), kv_send.at[step], kv_recv.at[step], (g, target, k)
        )
        copy.start()
        kv_copies.append(copy)

    pair = s + 1 - 2 * x
    other_base = (1 - x) * own_depth
    w_copies = []
    for tap in range(KW):
        copy = remote(
            wdec_hbm.at[tap, at(g * mid_depth, mid_depth, 16)],
            wdec.at[at(tap * width + x * own_depth + g * mid_depth, mid_depth, 16)],
            w_send.at[tap],
            w_recv.at[tap],
            (g, pair, k),
        )
        copy.start()
        w_copies.append(copy)
    wf_copies = []

    def pass_weight(tap):
        w_copies[tap].wait_recv()
        rows = wdec.at[at(tap * width + other_base + g * mid_depth, mid_depth, 16)]
        copy = remote(rows, rows, wf_send.at[tap], wf_recv.at[tap], (1 - g, s, k))
        copy.start()
        wf_copies.append(copy)

    loads[4].wait()
    queries = dot(normed, wq[...]).astype(jnp.bfloat16)
    queries = jnp.concatenate(
        [queries[:, i * HEAD : (i + 1) * HEAD] for i in range(heads)], axis=0
    )
    loads[3].wait()
    cells = bias_ref.shape[3]
    spreader = select_matrix(
        cells, keys, lambda i, j: jnp.logical_and(j >= PAIR * i, j < PAIR * i + PAIR)
    )
    for head in range(heads):
        rest = bias_ref[0, head]
        total = None
        for _ in range(3):
            term = rest.astype(jnp.bfloat16)
            rest = rest - term.astype(jnp.float32)
            wide = dot(term, spreader)
            total = wide if total is None else total + wide
        for cell in range(half // PAIR):
            first = head * half + cell * PAIR
            spread[first : first + PAIR, :] = jnp.broadcast_to(
                total[cell : cell + 1, :], (PAIR, keys)
            )

    kvf_copies = []
    for step in range(1, count):
        kv_copies[step - 1].wait_recv()
        source = lax.rem(s - step + count, count)
        copy = remote(
            kv_rows(source, k),
            kv_rows(source, k),
            kvf_send.at[step],
            kvf_recv.at[step],
            sibling,
        )
        copy.start()
        kvf_copies.append(copy)
    for copy in kvf_copies:
        copy.wait_recv()
    pass_weight(0)
    pass_weight(1)

    scores = lax.dot_general(
        queries,
        kv[:, :HEAD],
        (((1,), (1,)), ((), ())),
        preferred_element_type=jnp.float32,
    ) * (1.0 / math.sqrt(HEAD)) + spread[...]
    exponent = jnp.exp(scores - jnp.max(scores, axis=-1, keepdims=True))
    totals = jnp.sum(exponent, axis=-1, keepdims=True)
    context = (dot(exponent.astype(jnp.bfloat16), kv[:, HEAD:]) / totals).astype(jnp.bfloat16)
    context = jnp.concatenate([context[i * half : (i + 1) * half] for i in range(heads)], axis=1)
    loads[5].wait()
    partial[...] = dot(context, wout[...])

    part_out[...] = partial[at((1 - k) * quarter, quarter, 16), :].astype(jnp.bfloat16)
    part_copy = remote(part_out, part_in, sib_send.at[0], sib_recv.at[0], sibling)
    part_copy.start()
    pass_weight(2)
    pass_weight(3)
    part_copy.wait_recv()
    own = at(k * quarter, quarter, 16)
    attended = (
        pooled_ref[own, :] + (partial[own, :] + part_in[...].astype(jnp.float32))
    ).astype(jnp.bfloat16)
    repeater = select_matrix(
        half, quarter, lambda i, j: jnp.logical_or(i == 2 * j, i == 2 * j + 1)
    )
    own_rows = at(k * half, half, 16)
    joined = (dot(repeater, attended) + skip_ref[0, own_rows, :].astype(jnp.float32)).astype(
        jnp.bfloat16
    )
    loads[6].wait()
    activated = jax.nn.gelu(norm_scale(joined, dec_gain_ref[...][None, :])).astype(jnp.bfloat16)
    for chunk in range(pairs):
        act[chunk] = activated[:, chunk * width : (chunk + 1) * width]

    masks = sorted(range(1, pairs), key=lambda mask: (mask < pairs // 2, mask))

    def partner(mask):
        result = z
        bit = 1
        while bit < pairs:
            if mask & bit:
                result = result + bit * (1 - 2 * ((z // bit) % 2))
            bit *= 2
        return result

    edge_copies = []
    for mask in masks + [0]:
        target = partner(mask)
        for core in range(2):
            copy = remote(
                act.at[target, at(k * (half - 16), 16, 16)],
                edges.at[k, z],
                edge_send.at[mask * 2 + core],
                edge_recv.at[k, z],
                (g, target * 2 + 1 - x, core),
            )
            copy.start()
            edge_copies.append(copy)
    own_act = remote(
        act.at[z], gathered.at[z, own_rows], sib_send.at[1], sib_recv.at[1], sibling
    )
    own_act.start()
    act_copies = {}
    for step in masks:
        target = partner(step)
        copy = remote(
            act.at[target],
            gathered.at[z, own_rows],
            act_send.at[step],
            act_recv.at[step],
            (g, target * 2 + x, k),
        )
        copy.start()
        act_copies[step] = copy
    gathered[z, own_rows, :] = act[z]
    for section in range(2):
        resid_out[section] = joined[:, section * out_half : (section + 1) * out_half]
    resid_copy = remote(
        resid_out.at[1 - k], resid.at[own_rows], sib_send.at[2], sib_recv.at[2], sibling
    )
    resid_copy.start()
    resid[own_rows, :] = resid_out[k]

    actf_copies = {}

    def pass_act(step):
        act_copies[step].wait_recv()
        rows = gathered.at[partner(step), own_rows]
        copy = remote(rows, rows, actf_send.at[step], actf_recv.at[step], sibling)
        copy.start()
        actf_copies[step] = copy

    def convolve(block):
        low = edges[1, jnp.maximum(block - 1 + x, 0)].astype(jnp.float32)
        high = edges[0, jnp.minimum(block + x, pairs - 1)].astype(jnp.float32)
        padded[0:16, :] = jnp.where(block - 1 + x >= 0, low, 0.0)
        padded[16 : 16 + local_rows, :] = gathered[block].astype(jnp.float32)
        padded[16 + local_rows : 32 + local_rows, :] = jnp.where(block + x < pairs, high, 0.0)
        windows = []
        for tap in range(KW):
            first = 16 + tap - KW // 2
            windows.append(padded[first : first + local_rows, :].astype(jnp.bfloat16))
        return dot(jnp.concatenate(windows, axis=1), wdec[...])

    pass_weight(4)
    own_act.wait_recv()
    for core in range(2):
        for block in range(pairs):
            remote(
                act.at[0, pl.ds(0, 16)],
                edges.at[core, block],
                edge_send.at[0],
                edge_recv.at[core, block],
                sibling,
            ).wait_recv()
    for load in loads[7:]:
        load.wait()
    for copy in wf_copies:
        copy.wait_recv()
    pass_act(masks[0])
    result = convolve(z)
    conv_copies = []
    for step, mask in enumerate(masks):
        actf_copies[mask].wait_recv()
        if step + 1 < len(masks):
            pass_act(masks[step + 1])
        block = partner(mask)
        conv_out[step] = convolve(block).astype(jnp.bfloat16)
        copy = remote(
            conv_out.at[step],
            conv_in.at[step],
            conv_send.at[mask],
            conv_recv.at[mask],
            (g, block * 2 + x, k),
        )
        copy.start()
        conv_copies.append(copy)
    resid_copy.wait_recv()
    result = result + dec_bias_ref[...][None, :] + resid[...].astype(jnp.float32)
    for step, copy in enumerate(conv_copies):
        copy.wait_recv()
        result = result + conv_in[step].astype(jnp.float32)
    out_ref[...] = result.astype(jnp.bfloat16)
    for copy in (
        kv_copies
        + kvf_copies
        + w_copies
        + wf_copies
        + [part_copy, own_act, resid_copy]
        + edge_copies
        + list(act_copies.values())
        + list(actf_copies.values())
        + conv_copies
    ):
        copy.wait_send()


def fused_body(
    count,
    skip_in,
    attn_gain,
    query_weight,
    kv_weight,
    pair_bias,
    out_weight,
    dec_gain,
    dec_weight,
    dec_bias,
):
    _, local_rows, channels = skip_in.shape
    half = local_rows // 2
    quarter = half // 2
    pairs = count // 2
    width = channels // pairs
    heads = query_weight.shape[1] // HEAD
    out_half = dec_weight.shape[2]
    keys = half * count
    bf16, f32 = jnp.bfloat16, jnp.float32
    hbm = pl.BlockSpec(memory_space=pltpu.HBM)
    dma = pltpu.SemaphoreType.DMA
    scratch = [
        pltpu.VMEM(skip_in.shape, bf16),
        pltpu.VMEM(attn_gain.shape, f32),
        pltpu.VMEM(pair_bias.shape, f32),
        pltpu.VMEM(dec_gain.shape, f32),
        pltpu.VMEM(dec_bias.shape, f32),
        pltpu.VMEM(query_weight.shape, bf16),
        pltpu.VMEM(kv_weight.shape, bf16),
        pltpu.VMEM(out_weight.shape, bf16),
        pltpu.VMEM((KW * width, out_half), bf16),
        pltpu.VMEM((half, channels), f32),
        pltpu.VMEM((keys, 2 * HEAD), bf16),
        pltpu.VMEM((heads * half, keys), f32),
        pltpu.VMEM((half, channels), f32),
        pltpu.VMEM((quarter, channels), bf16),
        pltpu.VMEM((quarter, channels), bf16),
        pltpu.VMEM((pairs, half, width), bf16),
        pltpu.VMEM((pairs, local_rows, width), bf16),
        pltpu.VMEM((2, pairs, 16, width), bf16),
        pltpu.VMEM((local_rows + 32, width), f32),
        pltpu.VMEM((local_rows, out_half), bf16),
        pltpu.VMEM((2, half, out_half), bf16),
        pltpu.VMEM((pairs - 1, local_rows, out_half), bf16),
        pltpu.VMEM((pairs - 1, local_rows, out_half), bf16),
        dma((8 + KW,)),
        dma((count,)),
        dma((count,)),
        dma((count,)),
        dma((count,)),
        dma((KW,)),
        dma((KW,)),
        dma((KW,)),
        dma((KW,)),
        dma((3,)),
        dma((3,)),
        dma((pairs,)),
        dma((pairs,)),
        dma((pairs,)),
        dma((pairs,)),
        dma((2 * pairs,)),
        dma((2, pairs)),
        dma((pairs,)),
        dma((pairs,)),
    ]
    decoded = pl.pallas_call(
        functools.partial(block_kernel, count),
        out_shape=jax.ShapeDtypeStruct((local_rows, out_half), bf16),
        in_specs=[hbm] * 9,
        out_specs=pl.BlockSpec(memory_space=pltpu.VMEM),
        scratch_shapes=scratch,
        compiler_params=pltpu.CompilerParams(
            collective_id=0, has_side_effects=True, vmem_limit_bytes=63 * 1024 * 1024
        ),
        cost_estimate=pl.CostEstimate(
            flops=2 * local_rows * KW * channels * out_half,
            bytes_accessed=6_000_000,
            transcendentals=heads * half * keys,
        ),
    )(
        skip_in,
        attn_gain,
        query_weight,
        kv_weight,
        pair_bias,
        out_weight,
        dec_gain,
        dec_weight,
        dec_bias,
    )
    return decoded[None]


def solution(mesh):
    def chosen(skip_in, *others):
        fits = skip_in.shape[0] == 1 and skip_in.shape[1] % 64 == 0
        if fits and seq_pairs_fit(mesh, skip_in.shape[2]):
            return fused_body(mesh.shape["seq"], skip_in, *others)
        return body(skip_in, *others)

    return jax.shard_map(
        chosen,
        mesh=mesh,
        in_specs=(
            P("groups", "seq", None),
            P(),
            P(None, "section"),
            P(),
            P("groups", "section", "seq", None),
            P("section", None),
            P(),
            P(None, "seq", "section"),
            P("section"),
        ),
        out_specs=P("groups", "seq", "section"),
        check_vma=False,
    )
```

```python
import functools
import math

import jax
import jax.numpy as jnp
from jax import lax
from jax.experimental import pallas as pl
from jax.experimental.pallas import tpu as pltpu
from jax.sharding import PartitionSpec as P

HEAD = 128
KW = 5
PAIR = 16


def extended(block, sides, width):
    for axis, dim in sides:
        count = lax.axis_size(axis)
        forward = [(i, i + 1) for i in range(count - 1)]
        backward = [(target, source) for source, target in forward]
        low = lax.ppermute(
            lax.slice_in_dim(block, block.shape[dim] - width, None, axis=dim), axis, forward
        )
        high = lax.ppermute(lax.slice_in_dim(block, 0, width, axis=dim), axis, backward)
        block = jnp.concatenate([low, block, high], axis=dim)
    return block


def norm_scale(values_in, gain):
    wide = values_in.astype(jnp.float32)
    return wide * lax.rsqrt(jnp.mean(wide * wide, axis=-1, keepdims=True) + 1e-06) * gain


def body(
    skip_in,
    attn_gain,
    query_weight,
    kv_weight,
    pair_bias,
    out_weight,
    dec_gain,
    dec_weight,
    dec_bias,
):
    seq_count, local_rows, channels = skip_in.shape
    half_rows = local_rows // 2
    local_heads = query_weight.shape[1] // HEAD
    logit_scale = 1.0 / math.sqrt(HEAD)
    pooled = jnp.max(skip_in.reshape(seq_count, half_rows, 2, channels), axis=2)
    normed = norm_scale(pooled, attn_gain).astype(jnp.bfloat16)
    flattened = normed.reshape(seq_count * half_rows, channels)
    query_rows = jnp.dot(flattened, query_weight, preferred_element_type=jnp.float32).astype(
        jnp.bfloat16
    )
    query_rows = query_rows.reshape(seq_count, half_rows, local_heads, HEAD)
    row_bias = jnp.repeat(pair_bias, PAIR, axis=2)
    row_bias = jnp.pad(row_bias, ((0, 0), (0, 0), (0, 0), (0, 2)))
    quarter = half_rows // 2
    own_rows = lax.dynamic_slice_in_dim(normed, lax.axis_index("section") * quarter, quarter, 1)
    key_values = jnp.dot(
        own_rows.reshape(seq_count * quarter, channels),
        kv_weight,
        preferred_element_type=jnp.float32,
    )
    key_values = key_values.astype(jnp.bfloat16).reshape(seq_count, quarter, 2 * HEAD)
    piece = lax.all_gather(key_values, ("seq", "section"), axis=1, tiled=True)
    start = jnp.int32(0)
    running_max = jnp.full((seq_count, local_heads, half_rows), -1e30, jnp.float32)
    running_sum = jnp.zeros((seq_count, local_heads, half_rows), jnp.float32)
    weighted = jnp.zeros((seq_count, local_heads, half_rows, HEAD), jnp.float32)
    piece_rows = piece.shape[1]
    block_size = min(piece_rows, 2048)
    for offset in range(0, piece_rows, block_size):
        piece_len = min(block_size, piece_rows - offset)
        sub_piece = piece[:, offset : offset + piece_len]
        key_portion = sub_piece[:, :, :HEAD]
        value_part = sub_piece[:, :, HEAD:]
        first_row = start + offset
        blocks = lax.dynamic_slice_in_dim(row_bias, first_row // PAIR, piece_len // PAIR + 2, 3)
        spread = jnp.repeat(blocks, PAIR, axis=3)
        key_bias = lax.dynamic_slice_in_dim(spread, first_row % PAIR, piece_len, 3)
        scores = (
            jnp.einsum(
                "wtzj,wgj->wztg", query_rows, key_portion, preferred_element_type=jnp.float32
            )
            * logit_scale
            + key_bias
        )
        new_max = jnp.maximum(running_max, jnp.max(scores, axis=-1))
        rescale = jnp.exp(running_max - new_max)
        exponent_scores = jnp.exp(scores - new_max[..., None])
        running_sum = running_sum * rescale + jnp.sum(exponent_scores, axis=-1)
        weighted = weighted * rescale[..., None] + jnp.einsum(
            "umrl,ult->umrt",
            exponent_scores.astype(jnp.bfloat16),
            value_part,
            preferred_element_type=jnp.float32,
        )
        running_max = new_max
    folded = (running_max, running_sum, weighted)
    running_max, running_sum, weighted = folded
    context = (weighted / running_sum[..., None]).astype(jnp.bfloat16)
    context = jnp.transpose(context, (0, 2, 1, 3)).reshape(
        seq_count * half_rows, local_heads * HEAD
    )
    partial_value = jnp.dot(context, out_weight, preferred_element_type=jnp.float32).reshape(
        seq_count, half_rows, channels
    )
    summed = lax.psum(partial_value.astype(jnp.bfloat16), "section").astype(jnp.float32)
    attended = (pooled.astype(jnp.float32) + summed).astype(jnp.bfloat16)
    joined = (
        jnp.repeat(attended, 2, axis=1).astype(jnp.float32) + skip_in.astype(jnp.float32)
    ).astype(jnp.bfloat16)
    activated = jax.nn.gelu(norm_scale(joined, dec_gain)).astype(jnp.bfloat16)
    padded = extended(activated, (("seq", 1),), KW // 2)
    out_half = dec_weight.shape[2]
    piece = lax.all_gather(dec_weight, "seq", axis=1, tiled=True)
    piece_rows = piece.shape[1]
    stacked = jnp.concatenate(
        [padded[:, tap_index : tap_index + local_rows] for tap_index in range(KW)], axis=2
    )
    stacked = stacked.reshape(seq_count * local_rows, KW * piece_rows)
    convolved = jnp.dot(
        stacked, piece.reshape(KW * piece_rows, out_half), preferred_element_type=jnp.float32
    )
    residual = lax.dynamic_slice_in_dim(joined, lax.axis_index("section") * out_half, out_half, 2)
    decoded = (
        convolved.reshape(seq_count, local_rows, out_half) + dec_bias + residual.astype(jnp.float32)
    )
    return decoded.astype(jnp.bfloat16)


def seq_pairs_fit(mesh, channels):
    pairs = mesh.shape["seq"] // 2
    return (
        mesh.shape["groups"] == 2
        and mesh.shape["section"] == 2
        and mesh.shape["seq"] % 2 == 0
        and pairs >= 2
        and pairs & (pairs - 1) == 0
        and channels % (pairs * 128) == 0
    )


def dot(a, b):
    return jnp.dot(a, b, preferred_element_type=jnp.float32)


def select_matrix(rows, cols, chosen):
    i = lax.broadcasted_iota(jnp.int32, (rows, cols), 0)
    j = lax.broadcasted_iota(jnp.int32, (rows, cols), 1)
    return jnp.where(chosen(i, j), 1.0, 0.0).astype(jnp.bfloat16)


def block_kernel(
    count,
    skip_hbm,
    attn_gain_hbm,
    wq_hbm,
    wkv_hbm,
    bias_hbm,
    wout_hbm,
    dec_gain_hbm,
    wdec_hbm,
    dec_bias_hbm,
    out_ref,
    skip_ref,
    attn_gain_ref,
    bias_ref,
    dec_gain_ref,
    dec_bias_ref,
    wq,
    wkv,
    wout,
    wdec,
    pooled_ref,
    kv,
    spread,
    partial,
    part_out,
    part_in,
    act,
    gathered,
    edges,
    padded,
    resid,
    resid_out,
    conv_out,
    conv_in,
    local_sem,
    kv_send,
    kv_recv,
    kvf_send,
    kvf_recv,
    w_send,
    w_recv,
    wf_send,
    wf_recv,
    sib_send,
    sib_recv,
    act_send,
    act_recv,
    actf_send,
    actf_recv,
    edge_send,
    edge_recv,
    conv_send,
    conv_recv,
):
    g, s, k = lax.axis_index("groups"), lax.axis_index("seq"), lax.axis_index("section")
    pairs = count // 2
    z, x = s // 2, s % 2
    _, local_rows, channels = skip_hbm.shape
    half = local_rows // 2
    quarter = half // 2
    heads = wq.shape[1] // HEAD
    own_depth = wdec_hbm.shape[1]
    mid_depth = own_depth // 2
    out_half = wdec_hbm.shape[2]
    width = channels // pairs
    keys = kv.shape[0]
    sibling = (g, s, 1 - k)

    def remote(src, dst, send, recv, device):
        return pltpu.make_async_remote_copy(
            src_ref=src,
            dst_ref=dst,
            send_sem=send,
            recv_sem=recv,
            device_id=device,
            device_id_type=pl.DeviceIdType.MESH,
        )

    def at(start, size, step):
        return pl.ds(pl.multiple_of(start, step), size)

    sources = [
        (skip_hbm, skip_ref),
        (attn_gain_hbm, attn_gain_ref),
        (wkv_hbm, wkv),
        (bias_hbm, bias_ref),
        (wq_hbm, wq),
        (wout_hbm, wout),
        (dec_gain_hbm, dec_gain_ref),
        (dec_bias_hbm, dec_bias_ref),
    ] + [
        (wdec_hbm.at[tap], wdec.at[at(tap * width + x * own_depth, own_depth, 16)])
        for tap in range(KW)
    ]
    loads = [
        pltpu.make_async_copy(src, dst, local_sem.at[slot])
        for slot, (src, dst) in enumerate(sources)
    ]
    for load in loads[:3]:
        load.start()

    barrier = pltpu.get_barrier_semaphore()
    partners = [
        (g, lax.rem(s + step, count), lax.rem(k + core, 2))
        for step in range(count)
        for core in range(2)
        if step or core
    ] + [(1 - g, s, k)]
    for partner in partners:
        pl.semaphore_signal(
            barrier, inc=1, device_id=partner, device_id_type=pl.DeviceIdType.MESH
        )

    pl.semaphore_wait(barrier, len(partners))

    pair = s + 1 - 2 * x
    other_base = (1 - x) * own_depth
    w_copies = []
    for tap in range(KW):
        copy = remote(
            wdec_hbm.at[tap, at(g * mid_depth, mid_depth, 16)],
            wdec.at[at(tap * width + x * own_depth + g * mid_depth, mid_depth, 16)],
            w_send.at[tap],
            w_recv.at[tap],
            (g, pair, k),
        )
        copy.start()
        w_copies.append(copy)

    loads[0].wait()
    for load in loads[3:]:
        load.start()
    skip = skip_ref[0]
    pooled = jnp.maximum(
        dot(select_matrix(half, local_rows, lambda i, j: j == 2 * i), skip),
        dot(select_matrix(half, local_rows, lambda i, j: j == 2 * i + 1), skip),
    )
    pooled_ref[...] = pooled
    loads[1].wait()
    normed = norm_scale(pooled, attn_gain_ref[...][None, :]).astype(jnp.bfloat16)
    loads[2].wait()
    kv[at(s * half, half, 16), :] = dot(normed, wkv[...]).astype(jnp.bfloat16)

    def kv_rows(source, core):
        return kv.at[at(source * half + core * quarter, quarter, 16)]

    kv_copies = []
    for step in range(1, count):
        target = lax.rem(s + step, count)
        copy = remote(
            kv_rows(s, k), kv_rows(s, k), kv_send.at[step], kv_recv.at[step], (g, target, k)
        )
        copy.start()
        kv_copies.append(copy)

    wf_copies = []

    def pass_weight(tap):
        w_copies[tap].wait_recv()
        rows = wdec.at[at(tap * width + other_base + g * mid_depth, mid_depth, 16)]
        copy = remote(rows, rows, wf_send.at[tap], wf_recv.at[tap], (1 - g, s, k))
        copy.start()
        wf_copies.append(copy)

    loads[4].wait()
    queries = dot(normed, wq[...]).astype(jnp.bfloat16)
    queries = jnp.concatenate(
        [queries[:, i * HEAD : (i + 1) * HEAD] for i in range(heads)], axis=0
    )
    loads[3].wait()
    cells = bias_ref.shape[3]
    spreader = select_matrix(
        cells, keys, lambda i, j: jnp.logical_and(j >= PAIR * i, j < PAIR * i + PAIR)
    )
    for head in range(heads):
        rest = bias_ref[0, head]
        total = None
        for _ in range(3):
            term = rest.astype(jnp.bfloat16)
            rest = rest - term.astype(jnp.float32)
            wide = dot(term, spreader)
            total = wide if total is None else total + wide
        for cell in range(half // PAIR):
            first = head * half + cell * PAIR
            spread[first : first + PAIR, :] = jnp.broadcast_to(
                total[cell : cell + 1, :], (PAIR, keys)
            )

    kvf_copies = []
    for step in range(1, count):
        kv_copies[step - 1].wait_recv()
        source = lax.rem(s - step + count, count)
        copy = remote(
            kv_rows(source, k),
            kv_rows(source, k),
            kvf_send.at[step],
            kvf_recv.at[step],
            sibling,
        )
        copy.start()
        kvf_copies.append(copy)
    for copy in kvf_copies:
        copy.wait_recv()
    pass_weight(0)
    pass_weight(1)

    scores = lax.dot_general(
        queries,
        kv[:, :HEAD],
        (((1,), (1,)), ((), ())),
        preferred_element_type=jnp.float32,
    ) * (1.0 / math.sqrt(HEAD)) + spread[...]
    exponent = jnp.exp(scores - jnp.max(scores, axis=-1, keepdims=True))
    totals = jnp.sum(exponent, axis=-1, keepdims=True)
    context = (dot(exponent.astype(jnp.bfloat16), kv[:, HEAD:]) / totals).astype(jnp.bfloat16)
    context = jnp.concatenate([context[i * half : (i + 1) * half] for i in range(heads)], axis=1)
    loads[5].wait()
    partial[...] = dot(context, wout[...])

    part_out[...] = partial[at((1 - k) * quarter, quarter, 16), :].astype(jnp.bfloat16)
    part_copy = remote(part_out, part_in, sib_send.at[0], sib_recv.at[0], sibling)
    part_copy.start()
    pass_weight(2)
    part_copy.wait_recv()
    own = at(k * quarter, quarter, 16)
    attended = (
        pooled_ref[own, :] + (partial[own, :] + part_in[...].astype(jnp.float32))
    ).astype(jnp.bfloat16)
    repeater = select_matrix(
        half, quarter, lambda i, j: jnp.logical_or(i == 2 * j, i == 2 * j + 1)
    )
    own_rows = at(k * half, half, 16)
    joined = (dot(repeater, attended) + skip_ref[0, own_rows, :].astype(jnp.float32)).astype(
        jnp.bfloat16
    )
    loads[6].wait()
    activated = jax.nn.gelu(norm_scale(joined, dec_gain_ref[...][None, :])).astype(jnp.bfloat16)
    for chunk in range(pairs):
        act[chunk] = activated[:, chunk * width : (chunk + 1) * width]

    masks = sorted(range(1, pairs), key=lambda mask: (mask < pairs // 2, mask))

    def partner(mask):
        result = z
        bit = 1
        while bit < pairs:
            if mask & bit:
                result = result + bit * (1 - 2 * ((z // bit) % 2))
            bit *= 2
        return result

    edge_copies = []
    for mask in masks + [0]:
        target = partner(mask)
        for core in range(2):
            copy = remote(
                act.at[target, at(k * (half - 16), 16, 16)],
                edges.at[k, z],
                edge_send.at[mask * 2 + core],
                edge_recv.at[k, z],
                (g, target * 2 + 1 - x, core),
            )
            copy.start()
            edge_copies.append(copy)
    own_act = remote(
        act.at[z], gathered.at[z, own_rows], sib_send.at[1], sib_recv.at[1], sibling
    )
    own_act.start()
    act_copies = {}
    for step in masks:
        target = partner(step)
        copy = remote(
            act.at[target],
            gathered.at[z, own_rows],
            act_send.at[step],
            act_recv.at[step],
            (g, target * 2 + x, k),
        )
        copy.start()
        act_copies[step] = copy
    gathered[z, own_rows, :] = act[z]
    for section in range(2):
        resid_out[section] = joined[:, section * out_half : (section + 1) * out_half]
    resid_copy = remote(
        resid_out.at[1 - k], resid.at[own_rows], sib_send.at[2], sib_recv.at[2], sibling
    )
    resid_copy.start()
    resid[own_rows, :] = resid_out[k]

    actf_copies = {}

    def pass_act(step):
        act_copies[step].wait_recv()
        rows = gathered.at[partner(step), own_rows]
        copy = remote(rows, rows, actf_send.at[step], actf_recv.at[step], sibling)
        copy.start()
        actf_copies[step] = copy

    def convolve(block):
        low = edges[1, jnp.maximum(block - 1 + x, 0)].astype(jnp.float32)
        high = edges[0, jnp.minimum(block + x, pairs - 1)].astype(jnp.float32)
        padded[0:16, :] = jnp.where(block - 1 + x >= 0, low, 0.0)
        padded[16 : 16 + local_rows, :] = gathered[block].astype(jnp.float32)
        padded[16 + local_rows : 32 + local_rows, :] = jnp.where(block + x < pairs, high, 0.0)
        windows = []
        for tap in range(KW):
            first = 16 + tap - KW // 2
            windows.append(padded[first : first + local_rows, :].astype(jnp.bfloat16))
        return dot(jnp.concatenate(windows, axis=1), wdec[...])

    pass_weight(3)
    pass_weight(4)
    own_act.wait_recv()
    for core in range(2):
        for block in range(pairs):
            remote(
                act.at[0, pl.ds(0, 16)],
                edges.at[core, block],
                edge_send.at[0],
                edge_recv.at[core, block],
                sibling,
            ).wait_recv()
    for load in loads[7:]:
        load.wait()
    for copy in wf_copies:
        copy.wait_recv()
    pass_act(masks[0])
    result = convolve(z)
    conv_copies = []
    for step, mask in enumerate(masks):
        actf_copies[mask].wait_recv()
        if step + 1 < len(masks):
            pass_act(masks[step + 1])
        block = partner(mask)
        conv_out[step] = convolve(block).astype(jnp.bfloat16)
        copy = remote(
            conv_out.at[step],
            conv_in.at[step],
            conv_send.at[mask],
            conv_recv.at[mask],
            (g, block * 2 + x, k),
        )
        copy.start()
        conv_copies.append(copy)
    resid_copy.wait_recv()
    result = result + dec_bias_ref[...][None, :] + resid[...].astype(jnp.float32)
    for step, copy in enumerate(conv_copies):
        copy.wait_recv()
        result = result + conv_in[step].astype(jnp.float32)
    out_ref[...] = result.astype(jnp.bfloat16)
    for copy in (
        kv_copies
        + kvf_copies
        + w_copies
        + wf_copies
        + [part_copy, own_act, resid_copy]
        + edge_copies
        + list(act_copies.values())
        + list(actf_copies.values())
        + conv_copies
    ):
        copy.wait_send()


def fused_body(
    count,
    skip_in,
    attn_gain,
    query_weight,
    kv_weight,
    pair_bias,
    out_weight,
    dec_gain,
    dec_weight,
    dec_bias,
):
    _, local_rows, channels = skip_in.shape
    half = local_rows // 2
    quarter = half // 2
    pairs = count // 2
    width = channels // pairs
    heads = query_weight.shape[1] // HEAD
    out_half = dec_weight.shape[2]
    keys = half * count
    bf16, f32 = jnp.bfloat16, jnp.float32
    hbm = pl.BlockSpec(memory_space=pltpu.HBM)
    dma = pltpu.SemaphoreType.DMA
    scratch = [
        pltpu.VMEM(skip_in.shape, bf16),
        pltpu.VMEM(attn_gain.shape, f32),
        pltpu.VMEM(pair_bias.shape, f32),
        pltpu.VMEM(dec_gain.shape, f32),
        pltpu.VMEM(dec_bias.shape, f32),
        pltpu.VMEM(query_weight.shape, bf16),
        pltpu.VMEM(kv_weight.shape, bf16),
        pltpu.VMEM(out_weight.shape, bf16),
        pltpu.VMEM((KW * width, out_half), bf16),
        pltpu.VMEM((half, channels), f32),
        pltpu.VMEM((keys, 2 * HEAD), bf16),
        pltpu.VMEM((heads * half, keys), f32),
        pltpu.VMEM((half, channels), f32),
        pltpu.VMEM((quarter, channels), bf16),
        pltpu.VMEM((quarter, channels), bf16),
        pltpu.VMEM((pairs, half, width), bf16),
        pltpu.VMEM((pairs, local_rows, width), bf16),
        pltpu.VMEM((2, pairs, 16, width), bf16),
        pltpu.VMEM((local_rows + 32, width), f32),
        pltpu.VMEM((local_rows, out_half), bf16),
        pltpu.VMEM((2, half, out_half), bf16),
        pltpu.VMEM((pairs - 1, local_rows, out_half), bf16),
        pltpu.VMEM((pairs - 1, local_rows, out_half), bf16),
        dma((8 + KW,)),
        dma((count,)),
        dma((count,)),
        dma((count,)),
        dma((count,)),
        dma((KW,)),
        dma((KW,)),
        dma((KW,)),
        dma((KW,)),
        dma((3,)),
        dma((3,)),
        dma((pairs,)),
        dma((pairs,)),
        dma((pairs,)),
        dma((pairs,)),
        dma((2 * pairs,)),
        dma((2, pairs)),
        dma((pairs,)),
        dma((pairs,)),
    ]
    decoded = pl.pallas_call(
        functools.partial(block_kernel, count),
        out_shape=jax.ShapeDtypeStruct((local_rows, out_half), bf16),
        in_specs=[hbm] * 9,
        out_specs=pl.BlockSpec(memory_space=pltpu.VMEM),
        scratch_shapes=scratch,
        compiler_params=pltpu.CompilerParams(
            collective_id=0, has_side_effects=True, vmem_limit_bytes=63 * 1024 * 1024
        ),
        cost_estimate=pl.CostEstimate(
            flops=2 * local_rows * KW * channels * out_half,
            bytes_accessed=6_000_000,
            transcendentals=heads * half * keys,
        ),
    )(
        skip_in,
        attn_gain,
        query_weight,
        kv_weight,
        pair_bias,
        out_weight,
        dec_gain,
        dec_weight,
        dec_bias,
    )
    return decoded[None]


def solution(mesh):
    def chosen(skip_in, *others):
        fits = skip_in.shape[0] == 1 and skip_in.shape[1] % 64 == 0
        if fits and seq_pairs_fit(mesh, skip_in.shape[2]):
            return fused_body(mesh.shape["seq"], skip_in, *others)
        return body(skip_in, *others)

    return jax.shard_map(
        chosen,
        mesh=mesh,
        in_specs=(
            P("groups", "seq", None),
            P(),
            P(None, "section"),
            P(),
            P("groups", "section", "seq", None),
            P("section", None),
            P(),
            P(None, "seq", "section"),
            P("section"),
        ),
        out_specs=P("groups", "seq", "section"),
        check_vma=False,
    )
```

```python
import functools
import math

import jax
import jax.numpy as jnp
from jax import lax
from jax.experimental import pallas as pl
from jax.experimental.pallas import tpu as pltpu
from jax.sharding import PartitionSpec as P

HEAD = 128
KW = 5
PAIR = 16


def extended(block, sides, width):
    for axis, dim in sides:
        count = lax.axis_size(axis)
        forward = [(i, i + 1) for i in range(count - 1)]
        backward = [(target, source) for source, target in forward]
        low = lax.ppermute(
            lax.slice_in_dim(block, block.shape[dim] - width, None, axis=dim), axis, forward
        )
        high = lax.ppermute(lax.slice_in_dim(block, 0, width, axis=dim), axis, backward)
        block = jnp.concatenate([low, block, high], axis=dim)
    return block


def norm_scale(values_in, gain):
    wide = values_in.astype(jnp.float32)
    return wide * lax.rsqrt(jnp.mean(wide * wide, axis=-1, keepdims=True) + 1e-06) * gain


def body(
    skip_in,
    attn_gain,
    query_weight,
    kv_weight,
    pair_bias,
    out_weight,
    dec_gain,
    dec_weight,
    dec_bias,
):
    seq_count, local_rows, channels = skip_in.shape
    half_rows = local_rows // 2
    local_heads = query_weight.shape[1] // HEAD
    logit_scale = 1.0 / math.sqrt(HEAD)
    pooled = jnp.max(skip_in.reshape(seq_count, half_rows, 2, channels), axis=2)
    normed = norm_scale(pooled, attn_gain).astype(jnp.bfloat16)
    flattened = normed.reshape(seq_count * half_rows, channels)
    query_rows = jnp.dot(flattened, query_weight, preferred_element_type=jnp.float32).astype(
        jnp.bfloat16
    )
    query_rows = query_rows.reshape(seq_count, half_rows, local_heads, HEAD)
    row_bias = jnp.repeat(pair_bias, PAIR, axis=2)
    row_bias = jnp.pad(row_bias, ((0, 0), (0, 0), (0, 0), (0, 2)))
    quarter = half_rows // 2
    own_rows = lax.dynamic_slice_in_dim(normed, lax.axis_index("section") * quarter, quarter, 1)
    key_values = jnp.dot(
        own_rows.reshape(seq_count * quarter, channels),
        kv_weight,
        preferred_element_type=jnp.float32,
    )
    key_values = key_values.astype(jnp.bfloat16).reshape(seq_count, quarter, 2 * HEAD)
    piece = lax.all_gather(key_values, ("seq", "section"), axis=1, tiled=True)
    start = jnp.int32(0)
    running_max = jnp.full((seq_count, local_heads, half_rows), -1e30, jnp.float32)
    running_sum = jnp.zeros((seq_count, local_heads, half_rows), jnp.float32)
    weighted = jnp.zeros((seq_count, local_heads, half_rows, HEAD), jnp.float32)
    piece_rows = piece.shape[1]
    block_size = min(piece_rows, 2048)
    for offset in range(0, piece_rows, block_size):
        piece_len = min(block_size, piece_rows - offset)
        sub_piece = piece[:, offset : offset + piece_len]
        key_portion = sub_piece[:, :, :HEAD]
        value_part = sub_piece[:, :, HEAD:]
        first_row = start + offset
        blocks = lax.dynamic_slice_in_dim(row_bias, first_row // PAIR, piece_len // PAIR + 2, 3)
        spread = jnp.repeat(blocks, PAIR, axis=3)
        key_bias = lax.dynamic_slice_in_dim(spread, first_row % PAIR, piece_len, 3)
        scores = (
            jnp.einsum(
                "wtzj,wgj->wztg", query_rows, key_portion, preferred_element_type=jnp.float32
            )
            * logit_scale
            + key_bias
        )
        new_max = jnp.maximum(running_max, jnp.max(scores, axis=-1))
        rescale = jnp.exp(running_max - new_max)
        exponent_scores = jnp.exp(scores - new_max[..., None])
        running_sum = running_sum * rescale + jnp.sum(exponent_scores, axis=-1)
        weighted = weighted * rescale[..., None] + jnp.einsum(
            "umrl,ult->umrt",
            exponent_scores.astype(jnp.bfloat16),
            value_part,
            preferred_element_type=jnp.float32,
        )
        running_max = new_max
    folded = (running_max, running_sum, weighted)
    running_max, running_sum, weighted = folded
    context = (weighted / running_sum[..., None]).astype(jnp.bfloat16)
    context = jnp.transpose(context, (0, 2, 1, 3)).reshape(
        seq_count * half_rows, local_heads * HEAD
    )
    partial_value = jnp.dot(context, out_weight, preferred_element_type=jnp.float32).reshape(
        seq_count, half_rows, channels
    )
    summed = lax.psum(partial_value.astype(jnp.bfloat16), "section").astype(jnp.float32)
    attended = (pooled.astype(jnp.float32) + summed).astype(jnp.bfloat16)
    joined = (
        jnp.repeat(attended, 2, axis=1).astype(jnp.float32) + skip_in.astype(jnp.float32)
    ).astype(jnp.bfloat16)
    activated = jax.nn.gelu(norm_scale(joined, dec_gain)).astype(jnp.bfloat16)
    padded = extended(activated, (("seq", 1),), KW // 2)
    out_half = dec_weight.shape[2]
    piece = lax.all_gather(dec_weight, "seq", axis=1, tiled=True)
    piece_rows = piece.shape[1]
    stacked = jnp.concatenate(
        [padded[:, tap_index : tap_index + local_rows] for tap_index in range(KW)], axis=2
    )
    stacked = stacked.reshape(seq_count * local_rows, KW * piece_rows)
    convolved = jnp.dot(
        stacked, piece.reshape(KW * piece_rows, out_half), preferred_element_type=jnp.float32
    )
    residual = lax.dynamic_slice_in_dim(joined, lax.axis_index("section") * out_half, out_half, 2)
    decoded = (
        convolved.reshape(seq_count, local_rows, out_half) + dec_bias + residual.astype(jnp.float32)
    )
    return decoded.astype(jnp.bfloat16)


def seq_pairs_fit(mesh, channels):
    pairs = mesh.shape["seq"] // 2
    return (
        mesh.shape["groups"] == 2
        and mesh.shape["section"] == 2
        and mesh.shape["seq"] % 2 == 0
        and pairs >= 2
        and pairs & (pairs - 1) == 0
        and channels % (pairs * 128) == 0
    )


def dot(a, b):
    return jnp.dot(a, b, preferred_element_type=jnp.float32)


def select_matrix(rows, cols, chosen):
    i = lax.broadcasted_iota(jnp.int32, (rows, cols), 0)
    j = lax.broadcasted_iota(jnp.int32, (rows, cols), 1)
    return jnp.where(chosen(i, j), 1.0, 0.0).astype(jnp.bfloat16)


def block_kernel(
    count,
    skip_hbm,
    attn_gain_hbm,
    wq_hbm,
    wkv_hbm,
    bias_hbm,
    wout_hbm,
    dec_gain_hbm,
    wdec_hbm,
    dec_bias_hbm,
    out_ref,
    skip_ref,
    attn_gain_ref,
    bias_ref,
    dec_gain_ref,
    dec_bias_ref,
    wq,
    wkv,
    wout,
    wdec,
    pooled_ref,
    kv,
    spread,
    partial,
    part_out,
    part_in,
    act,
    gathered,
    edges,
    padded,
    resid,
    resid_out,
    conv_out,
    conv_in,
    local_sem,
    kv_send,
    kv_recv,
    kvf_send,
    kvf_recv,
    w_send,
    w_recv,
    wf_send,
    wf_recv,
    sib_send,
    sib_recv,
    act_send,
    act_recv,
    actf_send,
    actf_recv,
    edge_send,
    edge_recv,
    conv_send,
    conv_recv,
):
    g, s, k = lax.axis_index("groups"), lax.axis_index("seq"), lax.axis_index("section")
    pairs = count // 2
    z, x = s // 2, s % 2
    _, local_rows, channels = skip_hbm.shape
    half = local_rows // 2
    quarter = half // 2
    heads = wq.shape[1] // HEAD
    own_depth = wdec_hbm.shape[1]
    mid_depth = own_depth // 2
    out_half = wdec_hbm.shape[2]
    width = channels // pairs
    keys = kv.shape[0]
    sibling = (g, s, 1 - k)

    def remote(src, dst, send, recv, device):
        return pltpu.make_async_remote_copy(
            src_ref=src,
            dst_ref=dst,
            send_sem=send,
            recv_sem=recv,
            device_id=device,
            device_id_type=pl.DeviceIdType.MESH,
        )

    def at(start, size, step):
        return pl.ds(pl.multiple_of(start, step), size)

    sources = [
        (skip_hbm, skip_ref),
        (attn_gain_hbm, attn_gain_ref),
        (wkv_hbm, wkv),
        (bias_hbm, bias_ref),
        (wq_hbm, wq),
        (wout_hbm, wout),
        (dec_gain_hbm, dec_gain_ref),
        (dec_bias_hbm, dec_bias_ref),
    ] + [
        (wdec_hbm.at[tap], wdec.at[at(tap * width + x * own_depth, own_depth, 16)])
        for tap in range(KW)
    ]
    loads = [
        pltpu.make_async_copy(src, dst, local_sem.at[slot])
        for slot, (src, dst) in enumerate(sources)
    ]
    for load in loads[:3]:
        load.start()

    barrier = pltpu.get_barrier_semaphore()
    partners = [
        (g, lax.rem(s + step, count), lax.rem(k + core, 2))
        for step in range(count)
        for core in range(2)
        if step or core
    ] + [(1 - g, s, k)]
    for partner in partners:
        pl.semaphore_signal(
            barrier, inc=1, device_id=partner, device_id_type=pl.DeviceIdType.MESH
        )

    loads[0].wait()
    for load in loads[3:]:
        load.start()
    skip = skip_ref[0]
    pooled = jnp.maximum(
        dot(select_matrix(half, local_rows, lambda i, j: j == 2 * i), skip),
        dot(select_matrix(half, local_rows, lambda i, j: j == 2 * i + 1), skip),
    )
    pooled_ref[...] = pooled
    loads[1].wait()
    normed = norm_scale(pooled, attn_gain_ref[...][None, :]).astype(jnp.bfloat16)
    loads[2].wait()
    kv[at(s * half, half, 16), :] = dot(normed, wkv[...]).astype(jnp.bfloat16)

    pl.semaphore_wait(barrier, len(partners))

    def kv_rows(source, core):
        return kv.at[at(source * half + core * quarter, quarter, 16)]

    kv_copies = []
    for step in range(1, count):
        target = lax.rem(s + step, count)
        copy = remote(
            kv_rows(s, k), kv_rows(s, k), kv_send.at[step], kv_recv.at[step], (g, target, k)
        )
        copy.start()
        kv_copies.append(copy)

    pair = s + 1 - 2 * x
    other_base = (1 - x) * own_depth
    w_copies = []

    def send_weight(tap):
        copy = remote(
            wdec_hbm.at[tap, at(g * mid_depth, mid_depth, 16)],
            wdec.at[at(tap * width + x * own_depth + g * mid_depth, mid_depth, 16)],
            w_send.at[tap],
            w_recv.at[tap],
            (g, pair, k),
        )
        copy.start()
        w_copies.append(copy)

    wf_copies = []

    def pass_weight(tap):
        w_copies[tap].wait_recv()
        rows = wdec.at[at(tap * width + other_base + g * mid_depth, mid_depth, 16)]
        copy = remote(rows, rows, wf_send.at[tap], wf_recv.at[tap], (1 - g, s, k))
        copy.start()
        wf_copies.append(copy)

    loads[4].wait()
    queries = dot(normed, wq[...]).astype(jnp.bfloat16)
    queries = jnp.concatenate(
        [queries[:, i * HEAD : (i + 1) * HEAD] for i in range(heads)], axis=0
    )
    loads[3].wait()
    cells = bias_ref.shape[3]
    spreader = select_matrix(
        cells, keys, lambda i, j: jnp.logical_and(j >= PAIR * i, j < PAIR * i + PAIR)
    )
    for head in range(heads):
        rest = bias_ref[0, head]
        total = None
        for _ in range(3):
            term = rest.astype(jnp.bfloat16)
            rest = rest - term.astype(jnp.float32)
            wide = dot(term, spreader)
            total = wide if total is None else total + wide
        for cell in range(half // PAIR):
            first = head * half + cell * PAIR
            spread[first : first + PAIR, :] = jnp.broadcast_to(
                total[cell : cell + 1, :], (PAIR, keys)
            )

    kvf_copies = []
    for step in range(1, count):
        kv_copies[step - 1].wait_recv()
        source = lax.rem(s - step + count, count)
        copy = remote(
            kv_rows(source, k),
            kv_rows(source, k),
            kvf_send.at[step],
            kvf_recv.at[step],
            sibling,
        )
        copy.start()
        kvf_copies.append(copy)
    for tap in range(3):
        send_weight(tap)
    for copy in kvf_copies:
        copy.wait_recv()

    scores = lax.dot_general(
        queries,
        kv[:, :HEAD],
        (((1,), (1,)), ((), ())),
        preferred_element_type=jnp.float32,
    ) * (1.0 / math.sqrt(HEAD)) + spread[...]
    exponent = jnp.exp(scores - jnp.max(scores, axis=-1, keepdims=True))
    totals = jnp.sum(exponent, axis=-1, keepdims=True)
    context = (dot(exponent.astype(jnp.bfloat16), kv[:, HEAD:]) / totals).astype(jnp.bfloat16)
    context = jnp.concatenate([context[i * half : (i + 1) * half] for i in range(heads)], axis=1)
    loads[5].wait()
    partial[...] = dot(context, wout[...])

    part_out[...] = partial[at((1 - k) * quarter, quarter, 16), :].astype(jnp.bfloat16)
    part_copy = remote(part_out, part_in, sib_send.at[0], sib_recv.at[0], sibling)
    part_copy.start()
    for tap in range(3, KW):
        send_weight(tap)
    pass_weight(0)
    pass_weight(1)
    part_copy.wait_recv()
    own = at(k * quarter, quarter, 16)
    attended = (
        pooled_ref[own, :] + (partial[own, :] + part_in[...].astype(jnp.float32))
    ).astype(jnp.bfloat16)
    repeater = select_matrix(
        half, quarter, lambda i, j: jnp.logical_or(i == 2 * j, i == 2 * j + 1)
    )
    own_rows = at(k * half, half, 16)
    joined = (dot(repeater, attended) + skip_ref[0, own_rows, :].astype(jnp.float32)).astype(
        jnp.bfloat16
    )
    loads[6].wait()
    activated = jax.nn.gelu(norm_scale(joined, dec_gain_ref[...][None, :])).astype(jnp.bfloat16)
    for chunk in range(pairs):
        act[chunk] = activated[:, chunk * width : (chunk + 1) * width]

    masks = sorted(range(1, pairs), key=lambda mask: (mask < pairs // 2, mask))

    def partner(mask):
        result = z
        bit = 1
        while bit < pairs:
            if mask & bit:
                result = result + bit * (1 - 2 * ((z // bit) % 2))
            bit *= 2
        return result

    edge_copies = []
    for mask in masks + [0]:
        target = partner(mask)
        for core in range(2):
            copy = remote(
                act.at[target, at(k * (half - 16), 16, 16)],
                edges.at[k, z],
                edge_send.at[mask * 2 + core],
                edge_recv.at[k, z],
                (g, target * 2 + 1 - x, core),
            )
            copy.start()
            edge_copies.append(copy)
    own_act = remote(
        act.at[z], gathered.at[z, own_rows], sib_send.at[1], sib_recv.at[1], sibling
    )
    own_act.start()
    act_copies = {}
    for step in masks:
        target = partner(step)
        copy = remote(
            act.at[target],
            gathered.at[z, own_rows],
            act_send.at[step],
            act_recv.at[step],
            (g, target * 2 + x, k),
        )
        copy.start()
        act_copies[step] = copy
    gathered[z, own_rows, :] = act[z]
    for section in range(2):
        resid_out[section] = joined[:, section * out_half : (section + 1) * out_half]
    resid_copy = remote(
        resid_out.at[1 - k], resid.at[own_rows], sib_send.at[2], sib_recv.at[2], sibling
    )
    resid_copy.start()
    resid[own_rows, :] = resid_out[k]

    actf_copies = {}

    def pass_act(step):
        act_copies[step].wait_recv()
        rows = gathered.at[partner(step), own_rows]
        copy = remote(rows, rows, actf_send.at[step], actf_recv.at[step], sibling)
        copy.start()
        actf_copies[step] = copy

    def convolve(block):
        low = edges[1, jnp.maximum(block - 1 + x, 0)].astype(jnp.float32)
        high = edges[0, jnp.minimum(block + x, pairs - 1)].astype(jnp.float32)
        padded[0:16, :] = jnp.where(block - 1 + x >= 0, low, 0.0)
        padded[16 : 16 + local_rows, :] = gathered[block].astype(jnp.float32)
        padded[16 + local_rows : 32 + local_rows, :] = jnp.where(block + x < pairs, high, 0.0)
        windows = []
        for tap in range(KW):
            first = 16 + tap - KW // 2
            windows.append(padded[first : first + local_rows, :].astype(jnp.bfloat16))
        return dot(jnp.concatenate(windows, axis=1), wdec[...])

    for tap in range(2, KW):
        pass_weight(tap)
    own_act.wait_recv()
    for core in range(2):
        for block in range(pairs):
            remote(
                act.at[0, pl.ds(0, 16)],
                edges.at[core, block],
                edge_send.at[0],
                edge_recv.at[core, block],
                sibling,
            ).wait_recv()
    for load in loads[7:]:
        load.wait()
    for copy in wf_copies:
        copy.wait_recv()
    pass_act(masks[0])
    result = convolve(z)
    conv_copies = []
    for step, mask in enumerate(masks):
        actf_copies[mask].wait_recv()
        if step + 1 < len(masks):
            pass_act(masks[step + 1])
        block = partner(mask)
        conv_out[step] = convolve(block).astype(jnp.bfloat16)
        copy = remote(
            conv_out.at[step],
            conv_in.at[step],
            conv_send.at[mask],
            conv_recv.at[mask],
            (g, block * 2 + x, k),
        )
        copy.start()
        conv_copies.append(copy)
    resid_copy.wait_recv()
    result = result + dec_bias_ref[...][None, :] + resid[...].astype(jnp.float32)
    for step, copy in enumerate(conv_copies):
        copy.wait_recv()
        result = result + conv_in[step].astype(jnp.float32)
    out_ref[...] = result.astype(jnp.bfloat16)
    for copy in (
        kv_copies
        + kvf_copies
        + w_copies
        + wf_copies
        + [part_copy, own_act, resid_copy]
        + edge_copies
        + list(act_copies.values())
        + list(actf_copies.values())
        + conv_copies
    ):
        copy.wait_send()


def fused_body(
    count,
    skip_in,
    attn_gain,
    query_weight,
    kv_weight,
    pair_bias,
    out_weight,
    dec_gain,
    dec_weight,
    dec_bias,
):
    _, local_rows, channels = skip_in.shape
    half = local_rows // 2
    quarter = half // 2
    pairs = count // 2
    width = channels // pairs
    heads = query_weight.shape[1] // HEAD
    out_half = dec_weight.shape[2]
    keys = half * count
    bf16, f32 = jnp.bfloat16, jnp.float32
    hbm = pl.BlockSpec(memory_space=pltpu.HBM)
    dma = pltpu.SemaphoreType.DMA
    scratch = [
        pltpu.VMEM(skip_in.shape, bf16),
        pltpu.VMEM(attn_gain.shape, f32),
        pltpu.VMEM(pair_bias.shape, f32),
        pltpu.VMEM(dec_gain.shape, f32),
        pltpu.VMEM(dec_bias.shape, f32),
        pltpu.VMEM(query_weight.shape, bf16),
        pltpu.VMEM(kv_weight.shape, bf16),
        pltpu.VMEM(out_weight.shape, bf16),
        pltpu.VMEM((KW * width, out_half), bf16),
        pltpu.VMEM((half, channels), f32),
        pltpu.VMEM((keys, 2 * HEAD), bf16),
        pltpu.VMEM((heads * half, keys), f32),
        pltpu.VMEM((half, channels), f32),
        pltpu.VMEM((quarter, channels), bf16),
        pltpu.VMEM((quarter, channels), bf16),
        pltpu.VMEM((pairs, half, width), bf16),
        pltpu.VMEM((pairs, local_rows, width), bf16),
        pltpu.VMEM((2, pairs, 16, width), bf16),
        pltpu.VMEM((local_rows + 32, width), f32),
        pltpu.VMEM((local_rows, out_half), bf16),
        pltpu.VMEM((2, half, out_half), bf16),
        pltpu.VMEM((pairs - 1, local_rows, out_half), bf16),
        pltpu.VMEM((pairs - 1, local_rows, out_half), bf16),
        dma((8 + KW,)),
        dma((count,)),
        dma((count,)),
        dma((count,)),
        dma((count,)),
        dma((KW,)),
        dma((KW,)),
        dma((KW,)),
        dma((KW,)),
        dma((3,)),
        dma((3,)),
        dma((pairs,)),
        dma((pairs,)),
        dma((pairs,)),
        dma((pairs,)),
        dma((2 * pairs,)),
        dma((2, pairs)),
        dma((pairs,)),
        dma((pairs,)),
    ]
    decoded = pl.pallas_call(
        functools.partial(block_kernel, count),
        out_shape=jax.ShapeDtypeStruct((local_rows, out_half), bf16),
        in_specs=[hbm] * 9,
        out_specs=pl.BlockSpec(memory_space=pltpu.VMEM),
        scratch_shapes=scratch,
        compiler_params=pltpu.CompilerParams(
            collective_id=0, has_side_effects=True, vmem_limit_bytes=63 * 1024 * 1024
        ),
        cost_estimate=pl.CostEstimate(
            flops=2 * local_rows * KW * channels * out_half,
            bytes_accessed=6_000_000,
            transcendentals=heads * half * keys,
        ),
    )(
        skip_in,
        attn_gain,
        query_weight,
        kv_weight,
        pair_bias,
        out_weight,
        dec_gain,
        dec_weight,
        dec_bias,
    )
    return decoded[None]


def solution(mesh):
    def chosen(skip_in, *others):
        fits = skip_in.shape[0] == 1 and skip_in.shape[1] % 64 == 0
        if fits and seq_pairs_fit(mesh, skip_in.shape[2]):
            return fused_body(mesh.shape["seq"], skip_in, *others)
        return body(skip_in, *others)

    return jax.shard_map(
        chosen,
        mesh=mesh,
        in_specs=(
            P("groups", "seq", None),
            P(),
            P(None, "section"),
            P(),
            P("groups", "section", "seq", None),
            P("section", None),
            P(),
            P(None, "seq", "section"),
            P("section"),
        ),
        out_specs=P("groups", "seq", "section"),
        check_vma=False,
    )
```

```python
import functools
import math

import jax
import jax.numpy as jnp
from jax import lax
from jax.experimental import pallas as pl
from jax.experimental.pallas import tpu as pltpu
from jax.sharding import PartitionSpec as P

HEAD = 128
KW = 5
PAIR = 16


def extended(block, sides, width):
    for axis, dim in sides:
        count = lax.axis_size(axis)
        forward = [(i, i + 1) for i in range(count - 1)]
        backward = [(target, source) for source, target in forward]
        low = lax.ppermute(
            lax.slice_in_dim(block, block.shape[dim] - width, None, axis=dim), axis, forward
        )
        high = lax.ppermute(lax.slice_in_dim(block, 0, width, axis=dim), axis, backward)
        block = jnp.concatenate([low, block, high], axis=dim)
    return block


def norm_scale(values_in, gain):
    wide = values_in.astype(jnp.float32)
    return wide * lax.rsqrt(jnp.mean(wide * wide, axis=-1, keepdims=True) + 1e-06) * gain


def body(
    skip_in,
    attn_gain,
    query_weight,
    kv_weight,
    pair_bias,
    out_weight,
    dec_gain,
    dec_weight,
    dec_bias,
):
    seq_count, local_rows, channels = skip_in.shape
    half_rows = local_rows // 2
    local_heads = query_weight.shape[1] // HEAD
    logit_scale = 1.0 / math.sqrt(HEAD)
    pooled = jnp.max(skip_in.reshape(seq_count, half_rows, 2, channels), axis=2)
    normed = norm_scale(pooled, attn_gain).astype(jnp.bfloat16)
    flattened = normed.reshape(seq_count * half_rows, channels)
    query_rows = jnp.dot(flattened, query_weight, preferred_element_type=jnp.float32).astype(
        jnp.bfloat16
    )
    query_rows = query_rows.reshape(seq_count, half_rows, local_heads, HEAD)
    row_bias = jnp.repeat(pair_bias, PAIR, axis=2)
    row_bias = jnp.pad(row_bias, ((0, 0), (0, 0), (0, 0), (0, 2)))
    quarter = half_rows // 2
    own_rows = lax.dynamic_slice_in_dim(normed, lax.axis_index("section") * quarter, quarter, 1)
    key_values = jnp.dot(
        own_rows.reshape(seq_count * quarter, channels),
        kv_weight,
        preferred_element_type=jnp.float32,
    )
    key_values = key_values.astype(jnp.bfloat16).reshape(seq_count, quarter, 2 * HEAD)
    piece = lax.all_gather(key_values, ("seq", "section"), axis=1, tiled=True)
    start = jnp.int32(0)
    running_max = jnp.full((seq_count, local_heads, half_rows), -1e30, jnp.float32)
    running_sum = jnp.zeros((seq_count, local_heads, half_rows), jnp.float32)
    weighted = jnp.zeros((seq_count, local_heads, half_rows, HEAD), jnp.float32)
    piece_rows = piece.shape[1]
    block_size = min(piece_rows, 2048)
    for offset in range(0, piece_rows, block_size):
        piece_len = min(block_size, piece_rows - offset)
        sub_piece = piece[:, offset : offset + piece_len]
        key_portion = sub_piece[:, :, :HEAD]
        value_part = sub_piece[:, :, HEAD:]
        first_row = start + offset
        blocks = lax.dynamic_slice_in_dim(row_bias, first_row // PAIR, piece_len // PAIR + 2, 3)
        spread = jnp.repeat(blocks, PAIR, axis=3)
        key_bias = lax.dynamic_slice_in_dim(spread, first_row % PAIR, piece_len, 3)
        scores = (
            jnp.einsum(
                "wtzj,wgj->wztg", query_rows, key_portion, preferred_element_type=jnp.float32
            )
            * logit_scale
            + key_bias
        )
        new_max = jnp.maximum(running_max, jnp.max(scores, axis=-1))
        rescale = jnp.exp(running_max - new_max)
        exponent_scores = jnp.exp(scores - new_max[..., None])
        running_sum = running_sum * rescale + jnp.sum(exponent_scores, axis=-1)
        weighted = weighted * rescale[..., None] + jnp.einsum(
            "umrl,ult->umrt",
            exponent_scores.astype(jnp.bfloat16),
            value_part,
            preferred_element_type=jnp.float32,
        )
        running_max = new_max
    folded = (running_max, running_sum, weighted)
    running_max, running_sum, weighted = folded
    context = (weighted / running_sum[..., None]).astype(jnp.bfloat16)
    context = jnp.transpose(context, (0, 2, 1, 3)).reshape(
        seq_count * half_rows, local_heads * HEAD
    )
    partial_value = jnp.dot(context, out_weight, preferred_element_type=jnp.float32).reshape(
        seq_count, half_rows, channels
    )
    summed = lax.psum(partial_value.astype(jnp.bfloat16), "section").astype(jnp.float32)
    attended = (pooled.astype(jnp.float32) + summed).astype(jnp.bfloat16)
    joined = (
        jnp.repeat(attended, 2, axis=1).astype(jnp.float32) + skip_in.astype(jnp.float32)
    ).astype(jnp.bfloat16)
    activated = jax.nn.gelu(norm_scale(joined, dec_gain)).astype(jnp.bfloat16)
    padded = extended(activated, (("seq", 1),), KW // 2)
    out_half = dec_weight.shape[2]
    piece = lax.all_gather(dec_weight, "seq", axis=1, tiled=True)
    piece_rows = piece.shape[1]
    stacked = jnp.concatenate(
        [padded[:, tap_index : tap_index + local_rows] for tap_index in range(KW)], axis=2
    )
    stacked = stacked.reshape(seq_count * local_rows, KW * piece_rows)
    convolved = jnp.dot(
        stacked, piece.reshape(KW * piece_rows, out_half), preferred_element_type=jnp.float32
    )
    residual = lax.dynamic_slice_in_dim(joined, lax.axis_index("section") * out_half, out_half, 2)
    decoded = (
        convolved.reshape(seq_count, local_rows, out_half) + dec_bias + residual.astype(jnp.float32)
    )
    return decoded.astype(jnp.bfloat16)


def seq_pairs_fit(mesh, channels):
    pairs = mesh.shape["seq"] // 2
    return (
        mesh.shape["groups"] == 2
        and mesh.shape["section"] == 2
        and mesh.shape["seq"] % 2 == 0
        and pairs >= 2
        and pairs & (pairs - 1) == 0
        and channels % (pairs * 128) == 0
    )


def dot(a, b):
    return jnp.dot(a, b, preferred_element_type=jnp.float32)


def select_matrix(rows, cols, chosen):
    i = lax.broadcasted_iota(jnp.int32, (rows, cols), 0)
    j = lax.broadcasted_iota(jnp.int32, (rows, cols), 1)
    return jnp.where(chosen(i, j), 1.0, 0.0).astype(jnp.bfloat16)


def block_kernel(
    count,
    skip_hbm,
    attn_gain_hbm,
    wq_hbm,
    wkv_hbm,
    bias_hbm,
    wout_hbm,
    dec_gain_hbm,
    wdec_hbm,
    dec_bias_hbm,
    out_ref,
    skip_ref,
    attn_gain_ref,
    bias_ref,
    dec_gain_ref,
    dec_bias_ref,
    wq,
    wkv,
    wout,
    wdec,
    pooled_ref,
    kv,
    spread,
    partial,
    part_out,
    part_in,
    act,
    gathered,
    edges,
    padded,
    resid,
    resid_out,
    conv_out,
    conv_in,
    local_sem,
    kv_send,
    kv_recv,
    kvf_send,
    kvf_recv,
    w_send,
    w_recv,
    wf_send,
    wf_recv,
    sib_send,
    sib_recv,
    act_send,
    act_recv,
    actf_send,
    actf_recv,
    edge_send,
    edge_recv,
    conv_send,
    conv_recv,
):
    g, s, k = lax.axis_index("groups"), lax.axis_index("seq"), lax.axis_index("section")
    pairs = count // 2
    z, x = s // 2, s % 2
    _, local_rows, channels = skip_hbm.shape
    half = local_rows // 2
    quarter = half // 2
    heads = wq.shape[1] // HEAD
    own_depth = wdec_hbm.shape[1]
    mid_depth = own_depth // 2
    out_half = wdec_hbm.shape[2]
    width = channels // pairs
    keys = kv.shape[0]
    sibling = (g, s, 1 - k)

    def remote(src, dst, send, recv, device):
        return pltpu.make_async_remote_copy(
            src_ref=src,
            dst_ref=dst,
            send_sem=send,
            recv_sem=recv,
            device_id=device,
            device_id_type=pl.DeviceIdType.MESH,
        )

    def at(start, size, step):
        return pl.ds(pl.multiple_of(start, step), size)

    sources = [
        (skip_hbm, skip_ref),
        (attn_gain_hbm, attn_gain_ref),
        (wkv_hbm, wkv),
        (bias_hbm, bias_ref),
        (wq_hbm, wq),
        (wout_hbm, wout),
        (dec_gain_hbm, dec_gain_ref),
        (dec_bias_hbm, dec_bias_ref),
    ] + [
        (wdec_hbm.at[tap], wdec.at[at(tap * width + x * own_depth, own_depth, 16)])
        for tap in range(KW)
    ]
    loads = [
        pltpu.make_async_copy(src, dst, local_sem.at[slot])
        for slot, (src, dst) in enumerate(sources)
    ]
    for load in loads[:3]:
        load.start()

    barrier = pltpu.get_barrier_semaphore()
    partners = [
        (g, lax.rem(s + step, count), lax.rem(k + core, 2))
        for step in range(count)
        for core in range(2)
        if step or core
    ] + [(1 - g, s, k)]
    for partner in partners:
        pl.semaphore_signal(
            barrier, inc=1, device_id=partner, device_id_type=pl.DeviceIdType.MESH
        )

    loads[0].wait()
    for load in loads[3:]:
        load.start()
    skip = skip_ref[0]
    pooled = jnp.maximum(
        dot(select_matrix(half, local_rows, lambda i, j: j == 2 * i), skip),
        dot(select_matrix(half, local_rows, lambda i, j: j == 2 * i + 1), skip),
    )
    pooled_ref[...] = pooled
    loads[1].wait()
    normed = norm_scale(pooled, attn_gain_ref[...][None, :]).astype(jnp.bfloat16)
    loads[2].wait()
    kv[at(s * half, half, 16), :] = dot(normed, wkv[...]).astype(jnp.bfloat16)

    pl.semaphore_wait(barrier, len(partners))

    def kv_rows(source, core):
        return kv.at[at(source * half + core * quarter, quarter, 16)]

    kv_copies = []
    for step in range(1, count):
        target = lax.rem(s + step, count)
        copy = remote(
            kv_rows(s, k), kv_rows(s, k), kv_send.at[step], kv_recv.at[step], (g, target, k)
        )
        copy.start()
        kv_copies.append(copy)

    pair = s + 1 - 2 * x
    other_base = (1 - x) * own_depth
    w_copies = []
    for tap in range(KW):
        copy = remote(
            wdec_hbm.at[tap, at(g * mid_depth, mid_depth, 16)],
            wdec.at[at(tap * width + x * own_depth + g * mid_depth, mid_depth, 16)],
            w_send.at[tap],
            w_recv.at[tap],
            (g, pair, k),
        )
        copy.start()
        w_copies.append(copy)
    wf_copies = []

    def pass_weight(tap):
        w_copies[tap].wait_recv()
        rows = wdec.at[at(tap * width + other_base + g * mid_depth, mid_depth, 16)]
        copy = remote(rows, rows, wf_send.at[tap], wf_recv.at[tap], (1 - g, s, k))
        copy.start()
        wf_copies.append(copy)

    loads[4].wait()
    queries = dot(normed, wq[...]).astype(jnp.bfloat16)
    queries = jnp.concatenate(
        [queries[:, i * HEAD : (i + 1) * HEAD] for i in range(heads)], axis=0
    )
    loads[3].wait()
    cells = bias_ref.shape[3]
    spreader = select_matrix(
        cells, keys, lambda i, j: jnp.logical_and(j >= PAIR * i, j < PAIR * i + PAIR)
    )
    for head in range(heads):
        rest = bias_ref[0, head]
        total = None
        for _ in range(3):
            term = rest.astype(jnp.bfloat16)
            rest = rest - term.astype(jnp.float32)
            wide = dot(term, spreader)
            total = wide if total is None else total + wide
        for cell in range(half // PAIR):
            first = head * half + cell * PAIR
            spread[first : first + PAIR, :] = jnp.broadcast_to(
                total[cell : cell + 1, :], (PAIR, keys)
            )

    kvf_copies = []
    for step in range(1, count):
        kv_copies[step - 1].wait_recv()
        source = lax.rem(s - step + count, count)
        copy = remote(
            kv_rows(source, k),
            kv_rows(source, k),
            kvf_send.at[step],
            kvf_recv.at[step],
            sibling,
        )
        copy.start()
        kvf_copies.append(copy)
    for copy in kvf_copies:
        copy.wait_recv()
    pass_weight(0)
    pass_weight(1)

    scores = lax.dot_general(
        queries,
        kv[:, :HEAD],
        (((1,), (1,)), ((), ())),
        preferred_element_type=jnp.float32,
    ) * (1.0 / math.sqrt(HEAD)) + spread[...]
    exponent = jnp.exp(scores - jnp.max(scores, axis=-1, keepdims=True))
    totals = jnp.sum(exponent, axis=-1, keepdims=True)
    context = (dot(exponent.astype(jnp.bfloat16), kv[:, HEAD:]) / totals).astype(jnp.bfloat16)
    context = jnp.concatenate([context[i * half : (i + 1) * half] for i in range(heads)], axis=1)
    loads[5].wait()
    partial[...] = dot(context, wout[...])

    part_out[...] = partial[at((1 - k) * quarter, quarter, 16), :].astype(jnp.bfloat16)
    part_copy = remote(part_out, part_in, sib_send.at[0], sib_recv.at[0], sibling)
    part_copy.start()
    pass_weight(2)
    pass_weight(3)
    part_copy.wait_recv()
    own = at(k * quarter, quarter, 16)
    attended = (
        pooled_ref[own, :] + (partial[own, :] + part_in[...].astype(jnp.float32))
    ).astype(jnp.bfloat16)
    repeater = select_matrix(
        half, quarter, lambda i, j: jnp.logical_or(i == 2 * j, i == 2 * j + 1)
    )
    own_rows = at(k * half, half, 16)
    joined = (dot(repeater, attended) + skip_ref[0, own_rows, :].astype(jnp.float32)).astype(
        jnp.bfloat16
    )
    loads[6].wait()
    activated = jax.nn.gelu(norm_scale(joined, dec_gain_ref[...][None, :])).astype(jnp.bfloat16)
    for chunk in range(pairs):
        act[chunk] = activated[:, chunk * width : (chunk + 1) * width]

    masks = sorted(range(1, pairs), key=lambda mask: (mask < pairs // 2, mask))

    def partner(mask):
        result = z
        bit = 1
        while bit < pairs:
            if mask & bit:
                result = result + bit * (1 - 2 * ((z // bit) % 2))
            bit *= 2
        return result

    edge_copies = []
    for mask in masks + [0]:
        target = partner(mask)
        for core in range(2):
            copy = remote(
                act.at[target, at(k * (half - 16), 16, 16)],
                edges.at[k, z],
                edge_send.at[mask * 2 + core],
                edge_recv.at[k, z],
                (g, target * 2 + 1 - x, core),
            )
            copy.start()
            edge_copies.append(copy)
    own_act = remote(
        act.at[z], gathered.at[z, own_rows], sib_send.at[1], sib_recv.at[1], sibling
    )
    own_act.start()
    act_copies = {}
    for step in masks:
        target = partner(step)
        copy = remote(
            act.at[target],
            gathered.at[z, own_rows],
            act_send.at[step],
            act_recv.at[step],
            (g, target * 2 + x, k),
        )
        copy.start()
        act_copies[step] = copy
    gathered[z, own_rows, :] = act[z]
    for section in range(2):
        resid_out[section] = joined[:, section * out_half : (section + 1) * out_half]
    resid_copy = remote(
        resid_out.at[1 - k], resid.at[own_rows], sib_send.at[2], sib_recv.at[2], sibling
    )
    resid_copy.start()
    resid[own_rows, :] = resid_out[k]

    actf_copies = {}

    def pass_act(step):
        act_copies[step].wait_recv()
        rows = gathered.at[partner(step), own_rows]
        copy = remote(rows, rows, actf_send.at[step], actf_recv.at[step], sibling)
        copy.start()
        actf_copies[step] = copy

    def convolve(block, by_tap=False):
        low = edges[1, jnp.maximum(block - 1 + x, 0)].astype(jnp.float32)
        high = edges[0, jnp.minimum(block + x, pairs - 1)].astype(jnp.float32)
        padded[0:16, :] = jnp.where(block - 1 + x >= 0, low, 0.0)
        padded[16 : 16 + local_rows, :] = gathered[block].astype(jnp.float32)
        padded[16 + local_rows : 32 + local_rows, :] = jnp.where(block + x < pairs, high, 0.0)
        windows = []
        for tap in range(KW):
            first = 16 + tap - KW // 2
            windows.append(padded[first : first + local_rows, :].astype(jnp.bfloat16))
        if not by_tap:
            return dot(jnp.concatenate(windows, axis=1), wdec[...])
        total = None
        for tap in range(KW):
            wf_copies[tap].wait_recv()
            term = dot(windows[tap], wdec[tap * width : (tap + 1) * width])
            total = term if total is None else total + term
        return total

    pass_weight(4)
    own_act.wait_recv()
    for core in range(2):
        for block in range(pairs):
            remote(
                act.at[0, pl.ds(0, 16)],
                edges.at[core, block],
                edge_send.at[0],
                edge_recv.at[core, block],
                sibling,
            ).wait_recv()
    for load in loads[7:]:
        load.wait()
    pass_act(masks[0])
    result = convolve(z, by_tap=True)
    conv_copies = []
    for step, mask in enumerate(masks):
        actf_copies[mask].wait_recv()
        if step + 1 < len(masks):
            pass_act(masks[step + 1])
        block = partner(mask)
        conv_out[step] = convolve(block).astype(jnp.bfloat16)
        copy = remote(
            conv_out.at[step],
            conv_in.at[step],
            conv_send.at[mask],
            conv_recv.at[mask],
            (g, block * 2 + x, k),
        )
        copy.start()
        conv_copies.append(copy)
    resid_copy.wait_recv()
    result = result + dec_bias_ref[...][None, :] + resid[...].astype(jnp.float32)
    for step, copy in enumerate(conv_copies):
        copy.wait_recv()
        result = result + conv_in[step].astype(jnp.float32)
    out_ref[...] = result.astype(jnp.bfloat16)
    for copy in (
        kv_copies
        + kvf_copies
        + w_copies
        + wf_copies
        + [part_copy, own_act, resid_copy]
        + edge_copies
        + list(act_copies.values())
        + list(actf_copies.values())
        + conv_copies
    ):
        copy.wait_send()


def fused_body(
    count,
    skip_in,
    attn_gain,
    query_weight,
    kv_weight,
    pair_bias,
    out_weight,
    dec_gain,
    dec_weight,
    dec_bias,
):
    _, local_rows, channels = skip_in.shape
    half = local_rows // 2
    quarter = half // 2
    pairs = count // 2
    width = channels // pairs
    heads = query_weight.shape[1] // HEAD
    out_half = dec_weight.shape[2]
    keys = half * count
    bf16, f32 = jnp.bfloat16, jnp.float32
    hbm = pl.BlockSpec(memory_space=pltpu.HBM)
    dma = pltpu.SemaphoreType.DMA
    scratch = [
        pltpu.VMEM(skip_in.shape, bf16),
        pltpu.VMEM(attn_gain.shape, f32),
        pltpu.VMEM(pair_bias.shape, f32),
        pltpu.VMEM(dec_gain.shape, f32),
        pltpu.VMEM(dec_bias.shape, f32),
        pltpu.VMEM(query_weight.shape, bf16),
        pltpu.VMEM(kv_weight.shape, bf16),
        pltpu.VMEM(out_weight.shape, bf16),
        pltpu.VMEM((KW * width, out_half), bf16),
        pltpu.VMEM((half, channels), f32),
        pltpu.VMEM((keys, 2 * HEAD), bf16),
        pltpu.VMEM((heads * half, keys), f32),
        pltpu.VMEM((half, channels), f32),
        pltpu.VMEM((quarter, channels), bf16),
        pltpu.VMEM((quarter, channels), bf16),
        pltpu.VMEM((pairs, half, width), bf16),
        pltpu.VMEM((pairs, local_rows, width), bf16),
        pltpu.VMEM((2, pairs, 16, width), bf16),
        pltpu.VMEM((local_rows + 32, width), f32),
        pltpu.VMEM((local_rows, out_half), bf16),
        pltpu.VMEM((2, half, out_half), bf16),
        pltpu.VMEM((pairs - 1, local_rows, out_half), bf16),
        pltpu.VMEM((pairs - 1, local_rows, out_half), bf16),
        dma((8 + KW,)),
        dma((count,)),
        dma((count,)),
        dma((count,)),
        dma((count,)),
        dma((KW,)),
        dma((KW,)),
        dma((KW,)),
        dma((KW,)),
        dma((3,)),
        dma((3,)),
        dma((pairs,)),
        dma((pairs,)),
        dma((pairs,)),
        dma((pairs,)),
        dma((2 * pairs,)),
        dma((2, pairs)),
        dma((pairs,)),
        dma((pairs,)),
    ]
    decoded = pl.pallas_call(
        functools.partial(block_kernel, count),
        out_shape=jax.ShapeDtypeStruct((local_rows, out_half), bf16),
        in_specs=[hbm] * 9,
        out_specs=pl.BlockSpec(memory_space=pltpu.VMEM),
        scratch_shapes=scratch,
        compiler_params=pltpu.CompilerParams(
            collective_id=0, has_side_effects=True, vmem_limit_bytes=63 * 1024 * 1024
        ),
        cost_estimate=pl.CostEstimate(
            flops=2 * local_rows * KW * channels * out_half,
            bytes_accessed=6_000_000,
            transcendentals=heads * half * keys,
        ),
    )(
        skip_in,
        attn_gain,
        query_weight,
        kv_weight,
        pair_bias,
        out_weight,
        dec_gain,
        dec_weight,
        dec_bias,
    )
    return decoded[None]


def solution(mesh):
    def chosen(skip_in, *others):
        fits = skip_in.shape[0] == 1 and skip_in.shape[1] % 64 == 0
        if fits and seq_pairs_fit(mesh, skip_in.shape[2]):
            return fused_body(mesh.shape["seq"], skip_in, *others)
        return body(skip_in, *others)

    return jax.shard_map(
        chosen,
        mesh=mesh,
        in_specs=(
            P("groups", "seq", None),
            P(),
            P(None, "section"),
            P(),
            P("groups", "section", "seq", None),
            P("section", None),
            P(),
            P(None, "seq", "section"),
            P("section"),
        ),
        out_specs=P("groups", "seq", "section"),
        check_vma=False,
    )
```

```python
import functools
import math

import jax
import jax.numpy as jnp
from jax import lax
from jax.experimental import pallas as pl
from jax.experimental.pallas import tpu as pltpu
from jax.sharding import PartitionSpec as P

HEAD = 128
KW = 5
PAIR = 16


def extended(block, sides, width):
    for axis, dim in sides:
        count = lax.axis_size(axis)
        forward = [(i, i + 1) for i in range(count - 1)]
        backward = [(target, source) for source, target in forward]
        low = lax.ppermute(
            lax.slice_in_dim(block, block.shape[dim] - width, None, axis=dim), axis, forward
        )
        high = lax.ppermute(lax.slice_in_dim(block, 0, width, axis=dim), axis, backward)
        block = jnp.concatenate([low, block, high], axis=dim)
    return block


def norm_scale(values_in, gain):
    wide = values_in.astype(jnp.float32)
    return wide * lax.rsqrt(jnp.mean(wide * wide, axis=-1, keepdims=True) + 1e-06) * gain


def body(
    skip_in,
    attn_gain,
    query_weight,
    kv_weight,
    pair_bias,
    out_weight,
    dec_gain,
    dec_weight,
    dec_bias,
):
    seq_count, local_rows, channels = skip_in.shape
    half_rows = local_rows // 2
    local_heads = query_weight.shape[1] // HEAD
    logit_scale = 1.0 / math.sqrt(HEAD)
    pooled = jnp.max(skip_in.reshape(seq_count, half_rows, 2, channels), axis=2)
    normed = norm_scale(pooled, attn_gain).astype(jnp.bfloat16)
    flattened = normed.reshape(seq_count * half_rows, channels)
    query_rows = jnp.dot(flattened, query_weight, preferred_element_type=jnp.float32).astype(
        jnp.bfloat16
    )
    query_rows = query_rows.reshape(seq_count, half_rows, local_heads, HEAD)
    row_bias = jnp.repeat(pair_bias, PAIR, axis=2)
    row_bias = jnp.pad(row_bias, ((0, 0), (0, 0), (0, 0), (0, 2)))
    quarter = half_rows // 2
    own_rows = lax.dynamic_slice_in_dim(normed, lax.axis_index("section") * quarter, quarter, 1)
    key_values = jnp.dot(
        own_rows.reshape(seq_count * quarter, channels),
        kv_weight,
        preferred_element_type=jnp.float32,
    )
    key_values = key_values.astype(jnp.bfloat16).reshape(seq_count, quarter, 2 * HEAD)
    piece = lax.all_gather(key_values, ("seq", "section"), axis=1, tiled=True)
    start = jnp.int32(0)
    running_max = jnp.full((seq_count, local_heads, half_rows), -1e30, jnp.float32)
    running_sum = jnp.zeros((seq_count, local_heads, half_rows), jnp.float32)
    weighted = jnp.zeros((seq_count, local_heads, half_rows, HEAD), jnp.float32)
    piece_rows = piece.shape[1]
    block_size = min(piece_rows, 2048)
    for offset in range(0, piece_rows, block_size):
        piece_len = min(block_size, piece_rows - offset)
        sub_piece = piece[:, offset : offset + piece_len]
        key_portion = sub_piece[:, :, :HEAD]
        value_part = sub_piece[:, :, HEAD:]
        first_row = start + offset
        blocks = lax.dynamic_slice_in_dim(row_bias, first_row // PAIR, piece_len // PAIR + 2, 3)
        spread = jnp.repeat(blocks, PAIR, axis=3)
        key_bias = lax.dynamic_slice_in_dim(spread, first_row % PAIR, piece_len, 3)
        scores = (
            jnp.einsum(
                "wtzj,wgj->wztg", query_rows, key_portion, preferred_element_type=jnp.float32
            )
            * logit_scale
            + key_bias
        )
        new_max = jnp.maximum(running_max, jnp.max(scores, axis=-1))
        rescale = jnp.exp(running_max - new_max)
        exponent_scores = jnp.exp(scores - new_max[..., None])
        running_sum = running_sum * rescale + jnp.sum(exponent_scores, axis=-1)
        weighted = weighted * rescale[..., None] + jnp.einsum(
            "umrl,ult->umrt",
            exponent_scores.astype(jnp.bfloat16),
            value_part,
            preferred_element_type=jnp.float32,
        )
        running_max = new_max
    folded = (running_max, running_sum, weighted)
    running_max, running_sum, weighted = folded
    context = (weighted / running_sum[..., None]).astype(jnp.bfloat16)
    context = jnp.transpose(context, (0, 2, 1, 3)).reshape(
        seq_count * half_rows, local_heads * HEAD
    )
    partial_value = jnp.dot(context, out_weight, preferred_element_type=jnp.float32).reshape(
        seq_count, half_rows, channels
    )
    summed = lax.psum(partial_value.astype(jnp.bfloat16), "section").astype(jnp.float32)
    attended = (pooled.astype(jnp.float32) + summed).astype(jnp.bfloat16)
    joined = (
        jnp.repeat(attended, 2, axis=1).astype(jnp.float32) + skip_in.astype(jnp.float32)
    ).astype(jnp.bfloat16)
    activated = jax.nn.gelu(norm_scale(joined, dec_gain)).astype(jnp.bfloat16)
    padded = extended(activated, (("seq", 1),), KW // 2)
    out_half = dec_weight.shape[2]
    piece = lax.all_gather(dec_weight, "seq", axis=1, tiled=True)
    piece_rows = piece.shape[1]
    stacked = jnp.concatenate(
        [padded[:, tap_index : tap_index + local_rows] for tap_index in range(KW)], axis=2
    )
    stacked = stacked.reshape(seq_count * local_rows, KW * piece_rows)
    convolved = jnp.dot(
        stacked, piece.reshape(KW * piece_rows, out_half), preferred_element_type=jnp.float32
    )
    residual = lax.dynamic_slice_in_dim(joined, lax.axis_index("section") * out_half, out_half, 2)
    decoded = (
        convolved.reshape(seq_count, local_rows, out_half) + dec_bias + residual.astype(jnp.float32)
    )
    return decoded.astype(jnp.bfloat16)


def seq_pairs_fit(mesh, channels):
    pairs = mesh.shape["seq"] // 2
    return (
        mesh.shape["groups"] == 2
        and mesh.shape["section"] == 2
        and mesh.shape["seq"] % 2 == 0
        and pairs >= 2
        and pairs & (pairs - 1) == 0
        and channels % (pairs * 128) == 0
    )


def dot(a, b):
    return jnp.dot(a, b, preferred_element_type=jnp.float32)


def select_matrix(rows, cols, chosen):
    i = lax.broadcasted_iota(jnp.int32, (rows, cols), 0)
    j = lax.broadcasted_iota(jnp.int32, (rows, cols), 1)
    return jnp.where(chosen(i, j), 1.0, 0.0).astype(jnp.bfloat16)


def block_kernel(
    count,
    skip_hbm,
    attn_gain_hbm,
    wq_hbm,
    wkv_hbm,
    bias_hbm,
    wout_hbm,
    dec_gain_hbm,
    wdec_hbm,
    dec_bias_hbm,
    out_ref,
    skip_ref,
    attn_gain_ref,
    bias_ref,
    dec_gain_ref,
    dec_bias_ref,
    wq,
    wkv,
    wout,
    wdec,
    pooled_ref,
    kv,
    spread,
    partial,
    part_out,
    part_in,
    act,
    gathered,
    edges,
    padded,
    resid,
    resid_out,
    conv_out,
    conv_in,
    local_sem,
    kv_send,
    kv_recv,
    kvf_send,
    kvf_recv,
    w_send,
    w_recv,
    wf_send,
    wf_recv,
    sib_send,
    sib_recv,
    act_send,
    act_recv,
    actf_send,
    actf_recv,
    edge_send,
    edge_recv,
    conv_send,
    conv_recv,
):
    g, s, k = lax.axis_index("groups"), lax.axis_index("seq"), lax.axis_index("section")
    pairs = count // 2
    z, x = s // 2, s % 2
    _, local_rows, channels = skip_hbm.shape
    half = local_rows // 2
    quarter = half // 2
    heads = wq.shape[1] // HEAD
    own_depth = wdec_hbm.shape[1]
    mid_depth = own_depth // 2
    out_half = wdec_hbm.shape[2]
    width = channels // pairs
    keys = kv.shape[0]
    sibling = (g, s, 1 - k)

    def remote(src, dst, send, recv, device):
        return pltpu.make_async_remote_copy(
            src_ref=src,
            dst_ref=dst,
            send_sem=send,
            recv_sem=recv,
            device_id=device,
            device_id_type=pl.DeviceIdType.MESH,
        )

    def at(start, size, step):
        return pl.ds(pl.multiple_of(start, step), size)

    sources = [
        (skip_hbm, skip_ref),
        (attn_gain_hbm, attn_gain_ref),
        (wkv_hbm, wkv),
        (bias_hbm, bias_ref),
        (wq_hbm, wq),
        (wout_hbm, wout),
        (dec_gain_hbm, dec_gain_ref),
        (dec_bias_hbm, dec_bias_ref),
    ] + [
        (wdec_hbm.at[tap], wdec.at[at(tap * width + x * own_depth, own_depth, 16)])
        for tap in range(KW)
    ]
    loads = [
        pltpu.make_async_copy(src, dst, local_sem.at[slot])
        for slot, (src, dst) in enumerate(sources)
    ]
    for load in loads[:3]:
        load.start()

    barrier = pltpu.get_barrier_semaphore()
    partners = [
        (g, lax.rem(s + step, count), lax.rem(k + core, 2))
        for step in range(count)
        for core in range(2)
        if step or core
    ] + [(1 - g, s, k)]
    for partner in partners:
        pl.semaphore_signal(
            barrier, inc=1, device_id=partner, device_id_type=pl.DeviceIdType.MESH
        )

    loads[0].wait()
    for load in loads[3:]:
        load.start()
    skip = skip_ref[0]
    pooled = jnp.maximum(
        dot(select_matrix(half, local_rows, lambda i, j: j == 2 * i), skip),
        dot(select_matrix(half, local_rows, lambda i, j: j == 2 * i + 1), skip),
    )
    pooled_ref[...] = pooled
    loads[1].wait()
    normed = norm_scale(pooled, attn_gain_ref[...][None, :]).astype(jnp.bfloat16)
    loads[2].wait()
    kv[at(s * half, half, 16), :] = dot(normed, wkv[...]).astype(jnp.bfloat16)

    pl.semaphore_wait(barrier, len(partners))

    def kv_rows(source, core):
        return kv.at[at(source * half + core * quarter, quarter, 16)]

    kv_copies = []
    for step in range(1, count):
        target = lax.rem(s + step, count)
        copy = remote(
            kv_rows(s, k), kv_rows(s, k), kv_send.at[step], kv_recv.at[step], (g, target, k)
        )
        copy.start()
        kv_copies.append(copy)

    pair = s + 1 - 2 * x
    other_base = (1 - x) * own_depth
    w_copies = []

    def send_weight(tap):
        copy = remote(
            wdec_hbm.at[tap, at(g * mid_depth, mid_depth, 16)],
            wdec.at[at(tap * width + x * own_depth + g * mid_depth, mid_depth, 16)],
            w_send.at[tap],
            w_recv.at[tap],
            (g, pair, k),
        )
        copy.start()
        w_copies.append(copy)

    for tap in range(3):
        send_weight(tap)
    wf_copies = []

    def pass_weight(tap):
        w_copies[tap].wait_recv()
        rows = wdec.at[at(tap * width + other_base + g * mid_depth, mid_depth, 16)]
        copy = remote(rows, rows, wf_send.at[tap], wf_recv.at[tap], (1 - g, s, k))
        copy.start()
        wf_copies.append(copy)

    loads[4].wait()
    queries = dot(normed, wq[...]).astype(jnp.bfloat16)
    queries = jnp.concatenate(
        [queries[:, i * HEAD : (i + 1) * HEAD] for i in range(heads)], axis=0
    )
    loads[3].wait()
    cells = bias_ref.shape[3]
    spreader = select_matrix(
        cells, keys, lambda i, j: jnp.logical_and(j >= PAIR * i, j < PAIR * i + PAIR)
    )
    for head in range(heads):
        rest = bias_ref[0, head]
        total = None
        for _ in range(3):
            term = rest.astype(jnp.bfloat16)
            rest = rest - term.astype(jnp.float32)
            wide = dot(term, spreader)
            total = wide if total is None else total + wide
        for cell in range(half // PAIR):
            first = head * half + cell * PAIR
            spread[first : first + PAIR, :] = jnp.broadcast_to(
                total[cell : cell + 1, :], (PAIR, keys)
            )

    kvf_copies = []
    for step in range(1, count):
        kv_copies[step - 1].wait_recv()
        source = lax.rem(s - step + count, count)
        copy = remote(
            kv_rows(source, k),
            kv_rows(source, k),
            kvf_send.at[step],
            kvf_recv.at[step],
            sibling,
        )
        copy.start()
        kvf_copies.append(copy)
    for tap in range(3, KW):
        send_weight(tap)
    for copy in kvf_copies:
        copy.wait_recv()
    pass_weight(0)
    pass_weight(1)

    scores = lax.dot_general(
        queries,
        kv[:, :HEAD],
        (((1,), (1,)), ((), ())),
        preferred_element_type=jnp.float32,
    ) * (1.0 / math.sqrt(HEAD)) + spread[...]
    exponent = jnp.exp(scores - jnp.max(scores, axis=-1, keepdims=True))
    totals = jnp.sum(exponent, axis=-1, keepdims=True)
    context = (dot(exponent.astype(jnp.bfloat16), kv[:, HEAD:]) / totals).astype(jnp.bfloat16)
    context = jnp.concatenate([context[i * half : (i + 1) * half] for i in range(heads)], axis=1)
    loads[5].wait()
    partial[...] = dot(context, wout[...])

    part_out[...] = partial[at((1 - k) * quarter, quarter, 16), :].astype(jnp.bfloat16)
    part_copy = remote(part_out, part_in, sib_send.at[0], sib_recv.at[0], sibling)
    part_copy.start()
    pass_weight(2)
    pass_weight(3)
    part_copy.wait_recv()
    own = at(k * quarter, quarter, 16)
    attended = (
        pooled_ref[own, :] + (partial[own, :] + part_in[...].astype(jnp.float32))
    ).astype(jnp.bfloat16)
    repeater = select_matrix(
        half, quarter, lambda i, j: jnp.logical_or(i == 2 * j, i == 2 * j + 1)
    )
    own_rows = at(k * half, half, 16)
    joined = (dot(repeater, attended) + skip_ref[0, own_rows, :].astype(jnp.float32)).astype(
        jnp.bfloat16
    )
    loads[6].wait()
    activated = jax.nn.gelu(norm_scale(joined, dec_gain_ref[...][None, :])).astype(jnp.bfloat16)
    for chunk in range(pairs):
        act[chunk] = activated[:, chunk * width : (chunk + 1) * width]

    masks = sorted(range(1, pairs), key=lambda mask: (mask < pairs // 2, mask))

    def partner(mask):
        result = z
        bit = 1
        while bit < pairs:
            if mask & bit:
                result = result + bit * (1 - 2 * ((z // bit) % 2))
            bit *= 2
        return result

    edge_copies = []
    for mask in masks + [0]:
        target = partner(mask)
        for core in range(2):
            copy = remote(
                act.at[target, at(k * (half - 16), 16, 16)],
                edges.at[k, z],
                edge_send.at[mask * 2 + core],
                edge_recv.at[k, z],
                (g, target * 2 + 1 - x, core),
            )
            copy.start()
            edge_copies.append(copy)
    own_act = remote(
        act.at[z], gathered.at[z, own_rows], sib_send.at[1], sib_recv.at[1], sibling
    )
    own_act.start()
    act_copies = {}
    for step in masks:
        target = partner(step)
        copy = remote(
            act.at[target],
            gathered.at[z, own_rows],
            act_send.at[step],
            act_recv.at[step],
            (g, target * 2 + x, k),
        )
        copy.start()
        act_copies[step] = copy
    gathered[z, own_rows, :] = act[z]
    for section in range(2):
        resid_out[section] = joined[:, section * out_half : (section + 1) * out_half]
    resid_copy = remote(
        resid_out.at[1 - k], resid.at[own_rows], sib_send.at[2], sib_recv.at[2], sibling
    )
    resid_copy.start()
    resid[own_rows, :] = resid_out[k]

    actf_copies = {}

    def pass_act(step):
        act_copies[step].wait_recv()
        rows = gathered.at[partner(step), own_rows]
        copy = remote(rows, rows, actf_send.at[step], actf_recv.at[step], sibling)
        copy.start()
        actf_copies[step] = copy

    def convolve(block):
        low = edges[1, jnp.maximum(block - 1 + x, 0)].astype(jnp.float32)
        high = edges[0, jnp.minimum(block + x, pairs - 1)].astype(jnp.float32)
        padded[0:16, :] = jnp.where(block - 1 + x >= 0, low, 0.0)
        padded[16 : 16 + local_rows, :] = gathered[block].astype(jnp.float32)
        padded[16 + local_rows : 32 + local_rows, :] = jnp.where(block + x < pairs, high, 0.0)
        windows = []
        for tap in range(KW):
            first = 16 + tap - KW // 2
            windows.append(padded[first : first + local_rows, :].astype(jnp.bfloat16))
        return dot(jnp.concatenate(windows, axis=1), wdec[...])

    pass_weight(4)
    own_act.wait_recv()
    for core in range(2):
        for block in range(pairs):
            remote(
                act.at[0, pl.ds(0, 16)],
                edges.at[core, block],
                edge_send.at[0],
                edge_recv.at[core, block],
                sibling,
            ).wait_recv()
    for load in loads[7:]:
        load.wait()
    for copy in wf_copies:
        copy.wait_recv()
    pass_act(masks[0])
    result = convolve(z)
    conv_copies = []
    for step, mask in enumerate(masks):
        actf_copies[mask].wait_recv()
        if step + 1 < len(masks):
            pass_act(masks[step + 1])
        block = partner(mask)
        conv_out[step] = convolve(block).astype(jnp.bfloat16)
        copy = remote(
            conv_out.at[step],
            conv_in.at[step],
            conv_send.at[mask],
            conv_recv.at[mask],
            (g, block * 2 + x, k),
        )
        copy.start()
        conv_copies.append(copy)
    resid_copy.wait_recv()
    result = result + dec_bias_ref[...][None, :] + resid[...].astype(jnp.float32)
    for step, copy in enumerate(conv_copies):
        copy.wait_recv()
        result = result + conv_in[step].astype(jnp.float32)
    out_ref[...] = result.astype(jnp.bfloat16)
    for copy in (
        kv_copies
        + kvf_copies
        + w_copies
        + wf_copies
        + [part_copy, own_act, resid_copy]
        + edge_copies
        + list(act_copies.values())
        + list(actf_copies.values())
        + conv_copies
    ):
        copy.wait_send()


def fused_body(
    count,
    skip_in,
    attn_gain,
    query_weight,
    kv_weight,
    pair_bias,
    out_weight,
    dec_gain,
    dec_weight,
    dec_bias,
):
    _, local_rows, channels = skip_in.shape
    half = local_rows // 2
    quarter = half // 2
    pairs = count // 2
    width = channels // pairs
    heads = query_weight.shape[1] // HEAD
    out_half = dec_weight.shape[2]
    keys = half * count
    bf16, f32 = jnp.bfloat16, jnp.float32
    hbm = pl.BlockSpec(memory_space=pltpu.HBM)
    dma = pltpu.SemaphoreType.DMA
    scratch = [
        pltpu.VMEM(skip_in.shape, bf16),
        pltpu.VMEM(attn_gain.shape, f32),
        pltpu.VMEM(pair_bias.shape, f32),
        pltpu.VMEM(dec_gain.shape, f32),
        pltpu.VMEM(dec_bias.shape, f32),
        pltpu.VMEM(query_weight.shape, bf16),
        pltpu.VMEM(kv_weight.shape, bf16),
        pltpu.VMEM(out_weight.shape, bf16),
        pltpu.VMEM((KW * width, out_half), bf16),
        pltpu.VMEM((half, channels), f32),
        pltpu.VMEM((keys, 2 * HEAD), bf16),
        pltpu.VMEM((heads * half, keys), f32),
        pltpu.VMEM((half, channels), f32),
        pltpu.VMEM((quarter, channels), bf16),
        pltpu.VMEM((quarter, channels), bf16),
        pltpu.VMEM((pairs, half, width), bf16),
        pltpu.VMEM((pairs, local_rows, width), bf16),
        pltpu.VMEM((2, pairs, 16, width), bf16),
        pltpu.VMEM((local_rows + 32, width), f32),
        pltpu.VMEM((local_rows, out_half), bf16),
        pltpu.VMEM((2, half, out_half), bf16),
        pltpu.VMEM((pairs - 1, local_rows, out_half), bf16),
        pltpu.VMEM((pairs - 1, local_rows, out_half), bf16),
        dma((8 + KW,)),
        dma((count,)),
        dma((count,)),
        dma((count,)),
        dma((count,)),
        dma((KW,)),
        dma((KW,)),
        dma((KW,)),
        dma((KW,)),
        dma((3,)),
        dma((3,)),
        dma((pairs,)),
        dma((pairs,)),
        dma((pairs,)),
        dma((pairs,)),
        dma((2 * pairs,)),
        dma((2, pairs)),
        dma((pairs,)),
        dma((pairs,)),
    ]
    decoded = pl.pallas_call(
        functools.partial(block_kernel, count),
        out_shape=jax.ShapeDtypeStruct((local_rows, out_half), bf16),
        in_specs=[hbm] * 9,
        out_specs=pl.BlockSpec(memory_space=pltpu.VMEM),
        scratch_shapes=scratch,
        compiler_params=pltpu.CompilerParams(
            collective_id=0, has_side_effects=True, vmem_limit_bytes=63 * 1024 * 1024
        ),
        cost_estimate=pl.CostEstimate(
            flops=2 * local_rows * KW * channels * out_half,
            bytes_accessed=6_000_000,
            transcendentals=heads * half * keys,
        ),
    )(
        skip_in,
        attn_gain,
        query_weight,
        kv_weight,
        pair_bias,
        out_weight,
        dec_gain,
        dec_weight,
        dec_bias,
    )
    return decoded[None]


def solution(mesh):
    def chosen(skip_in, *others):
        fits = skip_in.shape[0] == 1 and skip_in.shape[1] % 64 == 0
        if fits and seq_pairs_fit(mesh, skip_in.shape[2]):
            return fused_body(mesh.shape["seq"], skip_in, *others)
        return body(skip_in, *others)

    return jax.shard_map(
        chosen,
        mesh=mesh,
        in_specs=(
            P("groups", "seq", None),
            P(),
            P(None, "section"),
            P(),
            P("groups", "section", "seq", None),
            P("section", None),
            P(),
            P(None, "seq", "section"),
            P("section"),
        ),
        out_specs=P("groups", "seq", "section"),
        check_vma=False,
    )
```
